256 devices in a mesh: seq: 16 (over z, core), expert: 16 (over y, x).
Axes of the slice: x: 4, y: 4, z: 8, core: 2. Of those that a mesh axis runs over, the one named last changes fastest.
Arguments:
- queries: bfloat16 [16, 2048, 4096], P('expert', 'seq')
- new_kv: bfloat16 [16, 2048, 2, 512], P('expert', 'seq'), may hold values from -6 to 6
- kv_pool: bfloat16 [8192, 8, 2, 512], P(('seq', 'expert')), may hold values from -6 to 6
- holders: int32 [16, 256], P('expert', 'seq'), may hold values from 0 to 15, as said below
- slots: int32 [16, 256], P('expert', 'seq'), may hold values from 0 to 31
- lengths: int32 [16], replicated, may hold values from 512 to 2048, as said below
- ssm_input: bfloat16 [16, 2048, 8192], P('expert', 'seq'), may hold values from -6 to 6
- step_sizes: float32 [16, 2048, 128], P('expert', 'seq'), may hold values from 0.3 to 2
- projections: float32 [16, 2048, 32], P('expert', 'seq'), may hold values from -1 to 1
- decay_rates: float32 [128], replicated, may hold values from 4.8828126e-05 to 0.05
- skip_gain: float32 [128], replicated, may hold values from 0.5 to 1.5
- init_state: float32 [16, 128, 1024], P('expert'), may hold values from -12 to 12
Outputs:
- attended: bfloat16 [16, 2048, 4096], P('expert', 'seq')
- ssm_out: bfloat16 [16, 2048, 8192], P('expert', 'seq')
The draws below stay inside these ranges and needn't reach their ends.
Inputs may be any that keep to these rules, and one draw needn't show every extreme that they name: `holders`: among the 16 blocks of one session on one index of seq no holder is named more than 2 times, and one holder exactly 2 times. `lengths`: in every draw one session holds exactly 2048 cached positions.
All inputs are finite; a program needn't handle non-finite values.
Results may differ from the reference program's by a relative error of at most 0.009.
Values may be sent and summed in bfloat16 or wider, within the bound.
A program may use at most 128 MiB of HBM per device.

```python
import math
from functools import partial
import jax
import jax.numpy as jnp
from jax import lax

Q_HEADS = 32
KV_HEADS = 4
HEAD_DIM = 128
SSM_HEADS = 128
SSM_DIM = 64
STATE = 16
TOK_DEV = 128
SESS = 16
TAIL = 2048
CTX = 2048
BLK = 8
POOL_DEV = 32
POOLS = 8192
CTXB = 256
N_SEQ = 16
N_EXPERT = 16


def draw_queries(key, part):
    key = jax.random.fold_in(key, 11)
    normal_key = jax.random.fold_in(key, 0)
    values = jax.random.normal(normal_key, (SESS, TAIL, Q_HEADS * HEAD_DIM), jnp.float32)
    return values.astype(jnp.bfloat16)


def draw_holders(key, part):
    key = jax.random.fold_in(key, 21)
    row_keys = jax.random.split(key, SESS * N_SEQ)

    def one_group(group_key):
        order_key, shuffle_key = jax.random.split(group_key)
        order = jax.random.permutation(order_key, N_EXPERT)
        picks = jnp.concatenate([order[:1], order[:N_EXPERT - 1]])
        return picks[jax.random.permutation(shuffle_key, N_EXPERT)]
    return jax.vmap(one_group)(row_keys).reshape(SESS, CTXB).astype(jnp.int32)


def draw_lengths(key, part):
    key = jax.random.fold_in(key, 31)
    value_key, which_key = jax.random.split(key)
    values = jax.random.randint(value_key, (SESS,), CTX // 4, CTX + 1, jnp.int32)
    chosen = jax.random.randint(which_key, (), 0, SESS, jnp.int32)
    return jnp.where(jnp.arange(SESS, dtype=jnp.int32) == chosen, CTX, values).astype(jnp.int32)


def with_ends(values, rng, smallest, top_value):
    dims = values.shape
    index_at = [jax.random.randint(jax.random.fold_in(rng, axis), (), 0, dims[axis]) for axis in range(len(dims))]
    values = values.at[tuple(index_at)].set(smallest)
    longest = dims.index(max(dims))
    index_at[longest] = (index_at[longest] + 1) % dims[longest]
    return values.at[tuple(index_at)].set(top_value)


def block_scale(stream_key, shape, cuts, least, largest):
    factor_of, own = 1.0, jax.random.fold_in(stream_key, 6)
    for position, parts in cuts:
        steps = jnp.exp(jax.random.uniform(jax.random.fold_in(own, position), (parts,), jnp.float32, least / len(cuts), largest / len(cuts)))
        factor_of = factor_of * jnp.repeat(steps, shape[position] // parts).reshape([-1 if axis == position else 1 for axis in range(len(shape))])
    return factor_of


def normal_values(own_key, shape, deviation, limit, shards=(), kind=jnp.bfloat16):
    loudness = block_scale(own_key, shape, shards, -0.22, 0.18) if shards else 1.0
    entries = jax.random.normal(own_key, shape, jnp.float32) * deviation * loudness
    return jnp.minimum(jnp.maximum(entries, -limit), limit).astype(kind)


def setup_inputs(seed: int = 0) -> dict:
    key_of = jax.random.split(jax.random.key(seed), 13)
    queries = draw_queries(jax.random.fold_in(key_of[12], 71), 0)
    new_kv = normal_values(key_of[1], (SESS, TAIL, 2, KV_HEADS * HEAD_DIM), 1.0, 6.0, ((0, 16), (1, 16)))
    kv_pool = normal_values(key_of[2], (POOLS, BLK, 2, KV_HEADS * HEAD_DIM), 1.0, 6.0, ((0, 256),))
    holders = draw_holders(jax.random.fold_in(key_of[12], 71), 0)
    slots = with_ends(jax.random.randint(key_of[4], (SESS, CTXB), 0, POOL_DEV), jax.random.fold_in(key_of[4], 1), 0, POOL_DEV - 1).astype(jnp.int32)
    lengths = draw_lengths(jax.random.fold_in(key_of[12], 71), 0)
    ssm_input = normal_values(key_of[6], (SESS, TAIL, SSM_HEADS * SSM_DIM), 1.0, 6.0, ((0, 16), (1, 16)))
    step_sizes = jnp.clip(jnp.exp(math.log(2.0) - 1.89712 * jax.random.uniform(key_of[7], (SESS, TAIL, SSM_HEADS), jnp.float32) ** block_scale(key_of[7], (SESS, TAIL, SSM_HEADS), ((0, 16), (1, 16)), -0.2, 0.2)), 0.3, 2.0)
    projections = normal_values(key_of[8], (SESS, TAIL, 2 * STATE), 0.15, 1.0, ((0, 16), (1, 16)), jnp.float32)
    decay_rates = jnp.clip(jnp.exp(jax.random.uniform(key_of[9], (SSM_HEADS,), jnp.float32, math.log(4.882812572759576e-05), math.log(0.05))), 4.882812572759576e-05, 0.05)
    skip_gain = jnp.clip(jax.random.uniform(key_of[10], (SSM_HEADS,), jnp.float32, 0.5, 1.5), 0.5, 1.5)
    init_state = normal_values(key_of[11], (SESS, SSM_HEADS, SSM_DIM * STATE), 2.0, 12.0, ((0, 16),), jnp.float32)
    return {"queries": queries, "new_kv": new_kv, "kv_pool": kv_pool, "holders": holders, "slots": slots, "lengths": lengths, "ssm_input": ssm_input, "step_sizes": step_sizes, "projections": projections, "decay_rates": decay_rates, "skip_gain": skip_gain, "init_state": init_state}


masked_score = -1e30


def reload_context(kv_pool, holders, slots):
    session_count, columns = holders.shape
    column_ids = jnp.arange(columns, dtype=jnp.int32)
    row_owner = (column_ids // N_EXPERT) * N_EXPERT
    pool_index = ((row_owner[None, :] + holders) * POOL_DEV + slots).astype(jnp.int32)
    gathered = kv_pool[pool_index]
    return gathered.reshape(session_count, columns * BLK, 2, gathered.shape[-1])


def attend_rows(query_rows, key_rows, visible):
    token_count = query_rows.shape[0]
    group_size = Q_HEADS // KV_HEADS
    query_float = query_rows.astype(jnp.float32).reshape(token_count, KV_HEADS, group_size, HEAD_DIM)
    key_float = key_rows[:, 0].astype(jnp.float32).reshape(-1, KV_HEADS, HEAD_DIM)
    value_float = key_rows[:, 1].astype(jnp.float32).reshape(-1, KV_HEADS, HEAD_DIM)
    scores = jnp.einsum('tkgd,skd->tkgs', query_float, key_float, precision=lax.Precision.HIGHEST) * (HEAD_DIM ** -0.5)
    shown_mask = visible[:, None, None, :]
    row_peak = jnp.max(jnp.where(shown_mask, scores, masked_score), axis=-1, keepdims=True)
    weights = jnp.where(shown_mask, jnp.exp(scores - row_peak), 0.0)
    totals = jnp.sum(weights, axis=-1)
    rounded = lax.optimization_barrier(weights.astype(jnp.bfloat16)).astype(jnp.float32)
    summed = jnp.einsum('tkgs,skd->tkgd', rounded, value_float, precision=lax.Precision.HIGHEST)
    return (summed / totals[..., None]).reshape(token_count, -1).astype(jnp.bfloat16)


def ssm_local(inputs, step_rows, write_rows, read_rows, decay_rates):
    row_count = inputs.shape[0]
    running_log = jnp.cumsum(-step_rows * decay_rates[None, :], axis=0)
    block_decay = running_log[-1]
    affinity = jnp.dot(read_rows, write_rows.T, precision=lax.Precision.HIGHEST)
    gaps = running_log[:, None, :] - running_log[None, :, :]
    causal = (jnp.arange(row_count, dtype=jnp.int32)[:, None] >= jnp.arange(row_count, dtype=jnp.int32)[None, :])[:, :, None]
    decays = jnp.where(causal, jnp.exp(jnp.minimum(gaps, 0.0)), 0.0)
    mixing = (affinity[:, :, None] * decays * step_rows[None, :, :]).astype(jnp.bfloat16)
    to_end = jnp.exp(block_decay[None, :] - running_log) * step_rows
    feeding = (to_end[:, :, None] * write_rows[:, None, :]).astype(jnp.bfloat16)
    return running_log, block_decay, feeding, mixing


def ssm_block(decay_rates, skip_gain, carried, block_rows):
    inputs, step_rows, projection_rows = block_rows
    row_count = inputs.shape[0]
    write_rows = projection_rows[:, :STATE]
    read_rows = projection_rows[:, STATE:]
    running_log, block_decay, feeding, mixing = ssm_local(inputs, step_rows, write_rows, read_rows, decay_rates)
    inner = inputs.astype(jnp.float32).reshape(row_count, SSM_HEADS, SSM_DIM)
    mixing_float = lax.optimization_barrier(mixing).astype(jnp.float32)
    feeding_float = lax.optimization_barrier(feeding).astype(jnp.float32)
    inside = jnp.einsum('tsh,shp->thp', mixing_float, inner, precision=lax.Precision.HIGHEST)
    block_end = jnp.einsum('shp,shn->hpn', inner, feeding_float, precision=lax.Precision.HIGHEST).reshape(SSM_HEADS, -1)
    outside = jnp.exp(running_log)[:, :, None] * jnp.einsum('hpn,tn->thp', carried.reshape(SSM_HEADS, SSM_DIM, STATE), read_rows, precision=lax.Precision.HIGHEST)
    result = (inside + outside + skip_gain[None, :, None] * inner).reshape(row_count, -1).astype(jnp.bfloat16)
    following = jnp.exp(block_decay)[:, None] * carried + block_end
    return following, result


def reference(queries, new_kv, kv_pool, holders, slots, lengths, ssm_input, step_sizes, projections, decay_rates, skip_gain, init_state):
    context = reload_context(kv_pool, holders, slots)
    key_index = jnp.arange(CTX + TAIL, dtype=jnp.int32)
    is_context = key_index < CTX

    def attend_session(session_rows):
        session_queries, session_new, session_context, session_length = session_rows
        key_rows = jnp.concatenate([session_context, session_new], axis=0)

        def attend_block(block_number):
            query_block = lax.dynamic_slice_in_dim(session_queries, block_number * TOK_DEV, TOK_DEV, 0)
            positions = block_number * TOK_DEV + jnp.arange(TOK_DEV, dtype=jnp.int32)
            visible = jnp.where(is_context[None, :], (key_index < session_length)[None, :], (key_index - CTX)[None, :] <= positions[:, None])
            return attend_rows(query_block, key_rows, visible)

        blocks = lax.map(attend_block, jnp.arange(TAIL // TOK_DEV, dtype=jnp.int32))
        return blocks.reshape(TAIL, -1)

    attended = lax.map(attend_session, (queries, new_kv, context, lengths))
    block_step = partial(ssm_block, decay_rates, skip_gain)

    def run_session(session_rows):
        session_input, session_steps, session_proj, session_state = session_rows
        block_rows = (session_input.reshape(TAIL // TOK_DEV, TOK_DEV, -1), session_steps.reshape(TAIL // TOK_DEV, TOK_DEV, -1), session_proj.reshape(TAIL // TOK_DEV, TOK_DEV, -1))
        final_state, outputs = lax.scan(block_step, session_state, block_rows)
        return outputs.reshape(TAIL, -1)

    ssm_out = lax.map(run_session, (ssm_input, step_sizes, projections, init_state))
    return attended, ssm_out
```

```python
import functools

import jax
import jax.numpy as jnp
from jax import lax
from jax.experimental import pallas as pl
from jax.experimental.pallas import tpu as pltpu
from jax.sharding import PartitionSpec as P

MESH = pl.DeviceIdType.MESH
BF = jnp.bfloat16
F32 = jnp.float32
I32 = jnp.int32
HIGH = lax.Precision.HIGHEST

KVH = 4
GRP = 8
DIM = 128
TOK = 128
NZ = 8
NEX = 16
UNIT = 256
HALF = 64
STATE = 16
CH = 8192
HCH = CH // 2
NSUB = 2
SUB = HCH // NSUB
SCALE = (DIM ** -0.5) * 1.4426950408889634
LOW = -1e30


def iota(shape, axis):
    return lax.broadcasted_iota(I32, shape, axis)


def kernel(
    q_ref, kv_ref, pool_ref, hold_ref, slot_ref, len_ref,
    x_ref, step_ref, proj_ref, decay_ref, skip_ref, init_ref,
    att_ref, ssm_ref,
    buf, qs, peak, acc, reqs, ids, picked, arrived, compact,
    xw, gain, dexp, sexp, ends, amat, plo,
    e_out, e_in, d_in, p_in, p_out, c_sib, c_in, carried,
    ksend, krecv, isend, irecv, bsend, brecv, esend, erecv, psend, precv, csend, crecv,
):
    me = lax.axis_index("seq")
    ex = lax.axis_index("expert")
    z = me // 2
    c = lax.rem(me, 2)
    right = lax.rem(z + 1, NZ) * 2 + c
    left = lax.rem(z + NZ - 1, NZ) * 2 + c
    sib = z * 2 + 1 - c

    barrier = pltpu.get_barrier_semaphore()
    for d in (right, left, sib):
        pl.semaphore_signal(barrier, inc=1, device_id=(d, ex), device_id_type=MESH)

    def greet(k, _):
        pl.semaphore_signal(
            barrier, inc=1, device_id=(me, lax.rem(ex + k, NEX)), device_id_type=MESH
        )
        return 0

    lax.fori_loop(1, NEX, greet, 0)

    spread = (iota((16, 128), 1) // 8 == iota((16, 128), 0)).astype(F32)
    hold = jnp.dot(hold_ref[...].astype(F32), spread, preferred_element_type=F32)
    slot = jnp.dot(slot_ref[...].astype(F32), spread, preferred_element_type=F32)
    row = iota((256, 128), 0)
    lane = iota((256, 128), 1)
    named = (hold[0:1] == (row // 16).astype(F32)).astype(F32)
    lead = ((iota((128, 128), 0) // 8 < iota((128, 128), 1) // 8)
            & (lax.rem(iota((128, 128), 0), 8) == 0)).astype(BF)
    before = jnp.dot(named.astype(BF), lead, preferred_element_type=F32)
    chosen = named * (before == lax.rem(row // 8, 2).astype(F32)).astype(F32)
    first = (lax.rem(lane, 8) == 0).astype(F32)
    wanted = jnp.sum(chosen * first * slot[0:1], axis=1, keepdims=True)
    reqs[...] = jnp.broadcast_to(wanted, (256, 128)).astype(I32)
    place = chosen * (lax.rem(row, 8) == lax.rem(lane, 8)).astype(F32)
    compact[...] = place.T.astype(BF)

    def where_rows(array, origin, half):
        return pl.ds(pl.multiple_of((array * 16 + origin) * TOK + half * HALF, HALF), HALF)

    def kv_copy(array, kind, s, half, origin, to):
        k = ((array * 4 + kind) * 5 + s) * 2 + half
        ref = buf.at[where_rows(array, origin, half)]
        return pltpu.make_async_remote_copy(
            src_ref=ref, dst_ref=ref, send_sem=ksend.at[k], recv_sem=krecv.at[k],
            device_id=(to, ex), device_id_type=MESH,
        )

    def right_origin(s):
        return lax.rem(z + NZ - s, NZ) * 2

    def left_origin(s):
        return lax.rem(z + s, NZ) * 2

    def send_own(array):
        for half in range(2):
            kv_copy(array, 0, 1, half, me, right).start()
            kv_copy(array, 1, 1, half, me, left).start()
        for half in range(2):
            kv_copy(array, 2, 0, half, me, sib).start()

    buf[where_rows(0, me, 0)] = kv_ref[0:HALF]
    buf[where_rows(0, me, 1)] = kv_ref[HALF:TOK]

    pl.semaphore_wait(barrier, 18)
    send_own(0)

    def ask(k, _):
        to = lax.rem(ex + k, NEX)
        pltpu.make_async_remote_copy(
            src_ref=reqs.at[pl.ds(pl.multiple_of(to * 16, 16), 16)],
            dst_ref=ids.at[pl.ds(pl.multiple_of(ex * 16, 16), 16)],
            send_sem=isend.at[k], recv_sem=irecv.at[k],
            device_id=(me, to), device_id_type=MESH,
        ).start()
        return 0

    lax.fori_loop(1, NEX, ask, 0)
    mine = pl.ds(pl.multiple_of(ex * 16, 16), 16)
    ids[mine] = reqs[mine]

    dec = decay_ref[...]
    steps = step_ref[...]
    lower = iota((128, 128), 0) >= iota((128, 128), 1)
    logs = jnp.dot(lower.astype(F32), -steps * dec, precision=HIGH, preferred_element_type=F32)
    total = logs[127:128]
    rows = jnp.concatenate(
        [
            jnp.exp(total - logs) * steps,
            jnp.exp(logs - total),
            jnp.broadcast_to(jnp.exp(total), (8, 128)),
            jnp.broadcast_to(skip_ref[...], (8, 128)),
        ],
        axis=0,
    )
    rows_hi = rows.astype(BF)
    rows_lo = (rows - rows_hi.astype(F32)).astype(BF)
    proj = proj_ref[...]
    proj_t = proj.T
    write_t = jnp.concatenate([jnp.zeros((STATE, 128), F32), proj_t[0:STATE]], axis=0)
    affinity = jnp.dot(proj, write_t, precision=HIGH, preferred_element_type=F32)
    amat[...] = jnp.where(lower, affinity, 0.0).astype(BF)
    plo[0] = proj.astype(BF)
    plo[1] = (proj - proj.astype(BF).astype(F32)).astype(BF)
    pt_hi = proj_t.astype(BF)
    pt_lo = (proj_t - pt_hi.astype(F32)).astype(BF)

    def widen(n, _):
        cols = pl.ds(pl.multiple_of(n * 256, 256), 256)
        one = (iota((128, 256), 0) == n * 4 + iota((128, 256), 1) // 64).astype(BF)
        wide = jnp.dot(rows_hi, one, preferred_element_type=F32) + jnp.dot(
            rows_lo, one, preferred_element_type=F32
        )
        fed = (x_ref[:, cols].astype(F32) * wide[0:128]).astype(BF)
        xw[:, cols] = fed
        gain[:, cols] = wide[128:256]
        dexp[:, cols] = wide[256:264]
        sexp[:, cols] = wide[264:272]
        end = jnp.dot(pt_hi, fed, preferred_element_type=F32) + jnp.dot(
            pt_lo, fed, preferred_element_type=F32
        )
        ends[:, cols] = end[0:STATE]
        return 0

    lax.fori_loop(0, CH // 256, widen, 0)

    my_half = pl.ds(pl.multiple_of(c * HCH, HCH), HCH)
    sib_half = pl.ds(pl.multiple_of((1 - c) * HCH, HCH), HCH)
    e_out[...] = ends[:, sib_half].astype(BF)

    def e_copy():
        return pltpu.make_async_remote_copy(
            src_ref=e_out, dst_ref=e_in, send_sem=esend.at[0], recv_sem=erecv.at[0],
            device_id=(sib, ex), device_id_type=MESH,
        )

    def d_copy():
        return pltpu.make_async_remote_copy(
            src_ref=dexp.at[:, sib_half], dst_ref=d_in, send_sem=esend.at[1],
            recv_sem=erecv.at[1], device_id=(sib, ex), device_id_type=MESH,
        )

    e_copy().start()
    d_copy().start()

    def ask_wait(k, _):
        source = pl.ds(pl.multiple_of(lax.rem(ex + NEX - k, NEX) * 16, 16), 16)
        pltpu.make_async_remote_copy(
            src_ref=ids.at[source], dst_ref=ids.at[source],
            send_sem=isend.at[k], recv_sem=irecv.at[k],
            device_id=(me, lax.rem(ex + k, NEX)), device_id_type=MESH,
        ).wait_recv()
        return 0

    lax.fori_loop(1, NEX, ask_wait, 0)
    got = ids[...]
    same = lax.rem(row, 8) == lax.rem(lane, 8)
    pick = jnp.concatenate(
        [
            ((got == lane // 8) & same).astype(BF),
            ((got == lane // 8 + 16) & same).astype(BF),
        ],
        axis=1,
    )
    picked[...] = jnp.dot(pick, pool_ref[...], preferred_element_type=F32).astype(BF)

    def block_copy(k):
        to = lax.rem(ex + k, NEX)
        return pltpu.make_async_remote_copy(
            src_ref=picked.at[pl.ds(pl.multiple_of(to * 16, 16), 16)],
            dst_ref=arrived.at[pl.ds(pl.multiple_of(ex * 16, 16), 16)],
            send_sem=bsend.at[k], recv_sem=brecv.at[k],
            device_id=(me, to), device_id_type=MESH,
        )

    def give(k, _):
        block_copy(k).start()
        return 0

    lax.fori_loop(1, NEX, give, 0)
    arrived[mine] = picked[mine]

    for g in range(KVH):
        for j in range(GRP):
            h = g * GRP + j
            qs[g, j * TOK:(j + 1) * TOK, :] = q_ref[:, h * DIM:(h + 1) * DIM]
    peak[...] = jnp.full_like(peak, LOW)
    acc[...] = jnp.zeros_like(acc)
    length = len_ref[ex]

    def attend(start, shown, bias):
        keep = iota((UNIT, DIM), 0) < shown
        one = keep.astype(F32).astype(BF)
        for g in range(KVH):
            kcols = slice(g * DIM, (g + 1) * DIM)
            vcols = slice(512 + g * DIM, 512 + (g + 1) * DIM)
            key = buf[pl.ds(start, UNIT), kcols]
            value = buf[pl.ds(start, UNIT), vcols]
            key = jnp.where(keep, key, jnp.broadcast_to(kv_ref[0:1, kcols], (UNIT, DIM)))
            value = value * one
            score = lax.dot_general(
                qs[g], key, (((1,), (1,)), ((), ())), preferred_element_type=F32
            )
            if bias is not None:
                score = score + bias
            old = peak[g]
            new = jnp.maximum(old, jnp.max(score, axis=1, keepdims=True))
            weight = jnp.exp2((score - jnp.concatenate([new, new], 1)) * SCALE).astype(BF)
            factor = jnp.exp2((old - new) * SCALE)
            acc[g] = acc[g] * jnp.concatenate([factor, factor], 1) + jnp.dot(
                weight, jnp.concatenate([value, one], axis=1), preferred_element_type=F32
            )
            peak[g] = new

    def sib_wait(array, kind, s, half):
        if kind == 0:
            origin = right_origin(s)
        else:
            origin = left_origin(s)
        kv_copy(array, 2 + kind, s, half, origin + 1 - c, sib).wait_recv()

    for half in range(2):
        kv_copy(0, 2, 0, half, sib, sib).wait_recv()
    token = lax.rem(iota((GRP * TOK, UNIT), 0), TOK) + c * TOK
    bias = jnp.where(iota((GRP * TOK, UNIT), 1) <= token, 0.0, LOW)
    attend(pl.multiple_of(z * UNIT, UNIT), UNIT, bias)

    def p_copy(k):
        return pltpu.make_async_remote_copy(
            src_ref=p_out.at[k], dst_ref=p_in.at[k], send_sem=psend.at[k],
            recv_sem=precv.at[k], device_id=(right, ex), device_id_type=MESH,
        )

    def c_copy(k):
        return pltpu.make_async_remote_copy(
            src_ref=c_sib.at[k], dst_ref=c_in.at[k], send_sem=csend.at[k],
            recv_sem=crecv.at[k], device_id=(sib, ex), device_id_type=MESH,
        )

    def chain():
        e_copy().wait_recv()
        d_copy().wait_recv()
        for k in range(NSUB):
            cols = pl.ds(pl.multiple_of(c * HCH + k * SUB, SUB), SUB)
            piece = slice(k * SUB, (k + 1) * SUB)

            @pl.when(z > 0)
            def _():
                p_copy(k).wait_recv()
                carried[:, cols] = p_in[k].astype(F32)

            @pl.when(z == 0)
            def _():
                carried[:, cols] = init_ref[:, cols]

            entering = carried[:, cols]
            own_e, own_d = ends[:, cols], dexp[0:1, cols]
            sib_e, sib_d = e_in[:, piece].astype(F32), d_in[0:1, piece]
            even = c == 0
            e0, e1 = jnp.where(even, own_e, sib_e), jnp.where(even, sib_e, own_e)
            d0, d1 = jnp.where(even, own_d, sib_d), jnp.where(even, sib_d, own_d)
            middle = d0 * entering + e0
            p_out[k] = (d1 * middle + e1).astype(BF)

            @pl.when(z < NZ - 1)
            def _():
                p_copy(k).start()

            c_sib[k] = jnp.where(even, middle, entering).astype(BF)
            c_copy(k).start()
            carried[:, cols] = jnp.where(even, entering, middle)

    def ssm_finish():
        for k in range(NSUB):
            c_copy(k).wait_recv()
            cols = pl.ds(pl.multiple_of((1 - c) * HCH + k * SUB, SUB), SUB)
            carried[:, cols] = c_in[k].astype(F32)

        def finish(n, _):
            cols = pl.ds(pl.multiple_of(n * 256, 256), 256)
            state = (carried[:, cols] * dexp[0:1, cols]).astype(BF)
            state = jnp.concatenate([jnp.zeros((STATE, 256), BF), state], axis=0)
            mixed = (
                jnp.dot(amat[...], xw[:, cols], preferred_element_type=F32)
                + jnp.dot(plo[0], state, preferred_element_type=F32)
                + jnp.dot(plo[1], state, preferred_element_type=F32)
            )
            ssm_ref[:, cols] = (
                gain[:, cols] * mixed + sexp[0:1, cols] * x_ref[:, cols].astype(F32)
            ).astype(BF)
            return 0

        lax.fori_loop(0, CH // 256, finish, 0)

    def assemble():
        def block_wait(k, _):
            source = pl.ds(pl.multiple_of(lax.rem(ex + NEX - k, NEX) * 16, 16), 16)
            pltpu.make_async_remote_copy(
                src_ref=arrived.at[source], dst_ref=arrived.at[source],
                send_sem=bsend.at[k], recv_sem=brecv.at[k],
                device_id=(me, lax.rem(ex + k, NEX)), device_id_type=MESH,
            ).wait_recv()
            return 0

        lax.fori_loop(1, NEX, block_wait, 0)
        context = jnp.dot(compact[...], arrived[...], preferred_element_type=F32).astype(BF)
        buf[where_rows(1, me, 0)] = context[0:HALF]
        buf[where_rows(1, me, 1)] = context[HALF:TOK]
        send_own(1)

    def stage(k):
        is_ctx = (k == 3) | (k >= 5)
        s = jnp.where(k < 3, k + 1, jnp.where(k == 3, 1, jnp.where(k == 4, 4, k - 3)))
        return jnp.where(is_ctx, 1, 0), s

    turn = 1 + (3 * z) // 2

    def step(it, _):
        k = it // 2
        j = lax.rem(it, 2)
        array, s = stage(k)
        last = 4 - j

        @pl.when(it == 3)
        def _():
            assemble()

        @pl.when(s <= last)
        def _():
            for kind in range(2):
                half = j if kind == 0 else 1 - j
                origin = (right_origin(s) if kind == 0 else left_origin(s)) + c
                kv_copy(array, kind, s, half, origin, sib).wait_recv()

                @pl.when(s < last)
                def _():
                    kv_copy(array, kind, s + 1, half, origin, right if kind == 0 else left).start()

                kv_copy(array, 2 + kind, s, half, origin, sib).start()

        @pl.when(it == turn)
        def _():
            chain()

        @pl.when(it == turn + 2)
        def _():
            ssm_finish()

        parray, ps = stage(k - 1)
        own = (k - 1 == 4) & (j == 1)
        uarray = jnp.where(own, 1, parray)
        chip = jnp.where(
            own, z, lax.rem(jnp.where(j == 0, z + NZ - ps, z + ps), NZ)
        )

        @pl.when(it >= 2)
        def _():
            @pl.when(own)
            def _():
                for half in range(2):
                    kv_copy(1, 2, 0, half, sib, sib).wait_recv()

            @pl.when(jnp.logical_not(own) & (ps < 4))
            def _():
                for half in range(2):
                    kv_copy(
                        parray, 2 + j, ps, half,
                        jnp.where(j == 0, right_origin(ps), left_origin(ps)) + 1 - c, sib,
                    ).wait_recv()

            @pl.when(jnp.logical_not(own) & (ps == 4))
            def _():
                sib_wait(parray, 0, 4, 0)
                sib_wait(parray, 1, 4, 1)

            @pl.when((uarray == 1) | (chip < z))
            def _():
                attend(
                    pl.multiple_of(uarray * 2048 + chip * UNIT, UNIT),
                    jnp.where(uarray == 1, length - chip * UNIT, UNIT),
                    None,
                )

        return 0

    lax.fori_loop(0, 16, step, 0)
    sib_wait(1, 0, 4, 0)
    sib_wait(1, 1, 4, 1)
    final = lax.rem(z + 4, NZ)
    attend(pl.multiple_of(2048 + final * UNIT, UNIT), length - final * UNIT, None)
    for g in range(KVH):
        sums = acc[g]
        done = (sums[:, 0:DIM] / sums[:, DIM:2 * DIM]).astype(BF)
        for j in range(GRP):
            h = g * GRP + j
            att_ref[:, h * DIM:(h + 1) * DIM] = done[j * TOK:(j + 1) * TOK]

    for array in range(2):
        for half in range(2):
            kv_copy(array, 2, 0, half, me, sib).wait_send()
            for kind in range(2):
                last = 4 if half == kind else 3
                to = right if kind == 0 else left
                for s in range(1, last + 1):
                    kv_copy(array, kind, s, half, me, to).wait_send()
                    kv_copy(array, 2 + kind, s, half, me, sib).wait_send()

    def drain(k, _):
        pltpu.make_async_remote_copy(
            src_ref=reqs.at[mine], dst_ref=ids.at[mine],
            send_sem=isend.at[k], recv_sem=irecv.at[k],
            device_id=(me, lax.rem(ex + k, NEX)), device_id_type=MESH,
        ).wait_send()
        block_copy(k).wait_send()
        return 0

    lax.fori_loop(1, NEX, drain, 0)
    e_copy().wait_send()
    d_copy().wait_send()
    for k in range(NSUB):
        c_copy(k).wait_send()

        @pl.when(z < NZ - 1)
        def _():
            p_copy(k).wait_send()


def local(
    queries, new_kv, kv_pool, holders, slots, lengths,
    ssm_input, step_sizes, projections, decay_rates, skip_gain, init_state,
):
    kv = new_kv[0].reshape(TOK, 1024)
    pool = kv_pool.reshape(256, 1024)
    state = init_state[0].reshape(CH, STATE).T
    vmem = pl.BlockSpec(memory_space=pltpu.VMEM)
    smem = pl.BlockSpec(memory_space=pltpu.SMEM)
    dma = pltpu.SemaphoreType.DMA
    attended, ssm_out = pl.pallas_call(
        kernel,
        out_shape=(
            jax.ShapeDtypeStruct((TOK, 4096), BF),
            jax.ShapeDtypeStruct((TOK, CH), BF),
        ),
        in_specs=[vmem] * 5 + [smem] + [vmem] * 6,
        out_specs=(vmem, vmem),
        scratch_shapes=[
            pltpu.VMEM((32 * TOK, 1024), BF),
            pltpu.VMEM((KVH, GRP * TOK, DIM), BF),
            pltpu.VMEM((KVH, GRP * TOK, DIM), F32),
            pltpu.VMEM((KVH, GRP * TOK, 2 * DIM), F32),
            pltpu.VMEM((256, 128), I32),
            pltpu.VMEM((256, 128), I32),
            pltpu.VMEM((256, 1024), BF),
            pltpu.VMEM((256, 1024), BF),
            pltpu.VMEM((128, 256), BF),
            pltpu.VMEM((TOK, CH), BF),
            pltpu.VMEM((TOK, CH), F32),
            pltpu.VMEM((8, CH), F32),
            pltpu.VMEM((8, CH), F32),
            pltpu.VMEM((STATE, CH), F32),
            pltpu.VMEM((128, 128), BF),
            pltpu.VMEM((2, 128, 32), BF),
            pltpu.VMEM((STATE, HCH), BF),
            pltpu.VMEM((STATE, HCH), BF),
            pltpu.VMEM((8, HCH), F32),
            pltpu.VMEM((NSUB, STATE, SUB), BF),
            pltpu.VMEM((NSUB, STATE, SUB), BF),
            pltpu.VMEM((NSUB, STATE, SUB), BF),
            pltpu.VMEM((NSUB, STATE, SUB), BF),
            pltpu.VMEM((STATE, CH), F32),
            dma((80,)), dma((80,)),
            dma((NEX,)), dma((NEX,)),
            dma((NEX,)), dma((NEX,)),
            dma((2,)), dma((2,)),
            dma((NSUB,)), dma((NSUB,)),
            dma((NSUB,)), dma((NSUB,)),
        ],
        compiler_params=pltpu.CompilerParams(
            vmem_limit_bytes=58 * 2 ** 20, collective_id=3, has_side_effects=True
        ),
        name="resume",
    )(
        queries[0], kv, pool, holders, slots, lengths,
        ssm_input[0], step_sizes[0], projections[0],
        decay_rates[None], skip_gain[None], state,
    )
    return attended[None], ssm_out[None]


def solution(mesh):
    placed = (
        P("expert", "seq", None),
        P("expert", "seq", None, None),
        P(("seq", "expert"), None, None, None),
        P("expert", "seq"),
        P("expert", "seq"),
        P(),
        P("expert", "seq", None),
        P("expert", "seq", None),
        P("expert", "seq", None),
        P(),
        P(),
        P("expert", None, None),
    )
    return jax.shard_map(
        local,
        mesh=mesh,
        in_specs=placed,
        out_specs=(P("expert", "seq", None), P("expert", "seq", None)),
        check_vma=False,
    )
```

```python
import functools

import jax
import jax.numpy as jnp
from jax import lax
from jax.experimental import pallas as pl
from jax.experimental.pallas import tpu as pltpu
from jax.sharding import PartitionSpec as P

MESH = pl.DeviceIdType.MESH
BF = jnp.bfloat16
F32 = jnp.float32
I32 = jnp.int32
HIGH = lax.Precision.HIGHEST

KVH = 4
GRP = 8
DIM = 128
TOK = 128
NZ = 8
NEX = 16
READY = 9
SIDE = 4
UNIT = 256
HALF = 64
STATE = 16
CH = 8192
HCH = CH // 2
WIDE = 1024
NSUB = 2
SUB = HCH // NSUB
SCALE = (DIM ** -0.5) * 1.4426950408889634
LOW = -1e30


def iota(shape, axis):
    return lax.broadcasted_iota(I32, shape, axis)


def kernel(
    q_hbm, kv_ref, pool_hbm, hold_ref, slot_ref, len_ref,
    x_hbm, step_ref, proj_ref, decay_ref, skip_ref, init_hbm,
    att_hbm, ssm_hbm,
    q_ref, pool_ref, x_ref, init_ref, att_ref, ssm_ref,
    buf, qs, peak, acc, reqs, middle_ids, ids, picked, arrived, compact,
    xw, gain, dexp, sexp, ends, amat, plo,
    e_out, e_in, d_in, p_in, p_out, c_sib, c_in, carried,
    ksend, krecv, isend, irecv, bsend, brecv, esend, erecv, psend, precv, csend, crecv, lsend,
):
    me = lax.axis_index("seq")
    ex = lax.axis_index("expert")
    z = me // 2
    c = lax.rem(me, 2)
    right = lax.rem(z + 1, NZ) * 2 + c
    left = lax.rem(z + NZ - 1, NZ) * 2 + c
    sib = z * 2 + 1 - c

    barrier = pltpu.get_barrier_semaphore()
    for d in (right, left, sib):
        pl.semaphore_signal(barrier, inc=1, device_id=(d, ex), device_id_type=MESH)

    ey, exx = ex // SIDE, lax.rem(ex, SIDE)

    def along_y(k):
        return lax.rem(ex + SIDE * k, NEX)

    def along_x(k):
        return ey * SIDE + lax.rem(exx + k, SIDE)

    def greet(k, _):
        pl.semaphore_signal(
            barrier, inc=1, device_id=(me, along_y(k)), device_id_type=MESH
        )
        pl.semaphore_signal(
            barrier, inc=1, device_id=(me, along_x(k)), device_id_type=MESH
        )
        return 0

    lax.fori_loop(1, SIDE, greet, 0)

    x_load = pltpu.make_async_copy(x_hbm, x_ref, lsend.at[0])
    q_load = pltpu.make_async_copy(q_hbm, q_ref, lsend.at[1])
    pool_load = pltpu.make_async_copy(pool_hbm, pool_ref, lsend.at[2])
    init_load = pltpu.make_async_copy(init_hbm, init_ref, lsend.at[3])
    att_store = pltpu.make_async_copy(att_ref, att_hbm, lsend.at[4])
    ssm_store = pltpu.make_async_copy(ssm_ref, ssm_hbm, lsend.at[5])
    x_load.start()
    pool_load.start()
    q_load.start()

    @pl.when(z == 0)
    def _():
        init_load.start()

    def where_rows(array, origin, half):
        return pl.ds(pl.multiple_of((array * 16 + origin) * TOK + half * HALF, HALF), HALF)

    def kv_copy(array, kind, s, half, origin, to):
        k = ((array * 4 + kind) * 5 + s) * 2 + half
        ref = buf.at[where_rows(array, origin, half)]
        return pltpu.make_async_remote_copy(
            src_ref=ref, dst_ref=ref, send_sem=ksend.at[0], recv_sem=krecv.at[k],
            device_id=(to, ex), device_id_type=MESH,
        )

    def right_origin(s):
        return lax.rem(z + NZ - s, NZ) * 2

    def left_origin(s):
        return lax.rem(z + s, NZ) * 2

    def send_own(array):
        for half in range(2):
            kv_copy(array, 0, 1, half, me, right).start()
            kv_copy(array, 1, 1, half, me, left).start()
        for half in range(2):
            kv_copy(array, 2, 0, half, me, sib).start()

    buf[where_rows(0, me, 0)] = kv_ref[0:HALF]
    buf[where_rows(0, me, 1)] = kv_ref[HALF:TOK]

    spread = (iota((16, 128), 1) // 8 == iota((16, 128), 0)).astype(F32)
    hold = jnp.dot(hold_ref[...].astype(F32), spread, preferred_element_type=F32)
    slot = jnp.dot(slot_ref[...].astype(F32), spread, preferred_element_type=F32)
    row = iota((256, 128), 0)
    lane = iota((256, 128), 1)
    named = (hold[0:1] == (row // 16).astype(F32)).astype(F32)
    lead = ((iota((128, 128), 0) // 8 < iota((128, 128), 1) // 8)
            & (lax.rem(iota((128, 128), 0), 8) == 0)).astype(BF)
    before = jnp.dot(named.astype(BF), lead, preferred_element_type=F32)
    chosen = named * (before == lax.rem(row // 8, 2).astype(F32)).astype(F32)
    first = (lax.rem(lane, 8) == 0).astype(F32)
    wanted = jnp.sum(chosen * first * slot[0:1], axis=1, keepdims=True)
    reqs[...] = jnp.broadcast_to(wanted, (256, 128)).astype(I32).reshape(SIDE, 64, 128)
    place = chosen * (lax.rem(row, 8) == lax.rem(lane, 8)).astype(F32)
    compact[...] = place.T.astype(BF)

    pl.semaphore_wait(barrier, 9)
    send_own(0)


    def ask_y(k, _):
        to = along_y(k)
        pltpu.make_async_remote_copy(
            src_ref=reqs.at[to // SIDE], dst_ref=middle_ids.at[ey],
            send_sem=isend.at[0], recv_sem=irecv.at[0],
            device_id=(me, to), device_id_type=MESH,
        ).start()
        return 0

    lax.fori_loop(1, SIDE, ask_y, 0)
    middle_ids[ey] = reqs[ey]
    mine_x = pl.ds(pl.multiple_of(exx * 16, 16), 16)
    mine = pl.ds(pl.multiple_of(ex * 16, 16), 16)

    dec = decay_ref[...]
    steps = step_ref[...]
    lower = iota((128, 128), 0) >= iota((128, 128), 1)
    logs = jnp.dot(lower.astype(F32), -steps * dec, precision=HIGH, preferred_element_type=F32)
    total = logs[127:128]
    rows = jnp.concatenate(
        [
            jnp.exp(total - logs) * steps,
            jnp.exp(logs - total),
            jnp.broadcast_to(jnp.exp(total), (8, 128)),
            jnp.broadcast_to(skip_ref[...], (8, 128)),
        ],
        axis=0,
    )
    rows_hi = rows.astype(BF)
    rows_cat = jnp.concatenate([rows_hi, (rows - rows_hi.astype(F32)).astype(BF)], axis=1)
    proj_t = proj_ref[...]
    proj = proj_t.T
    write_t = jnp.concatenate([jnp.zeros((STATE, 128), F32), proj_t[0:STATE]], axis=0)
    affinity = jnp.dot(proj, write_t, precision=HIGH, preferred_element_type=F32)
    amat[...] = jnp.where(lower, affinity, 0.0).astype(BF)
    plo[0] = proj.astype(BF)
    plo[1] = (proj - proj.astype(BF).astype(F32)).astype(BF)
    pt_hi = proj_t.astype(BF)
    pt_lo = (proj_t - pt_hi.astype(F32)).astype(BF)

    x_load.wait()

    def widen(n, _):
        cols = pl.ds(pl.multiple_of(n * WIDE, WIDE), WIDE)
        one = (iota((128, WIDE), 0) == n * (WIDE // 64) + iota((128, WIDE), 1) // 64)
        one = one.astype(BF)
        wide = jnp.dot(
            rows_cat, jnp.concatenate([one, one], axis=0), preferred_element_type=F32
        )
        fed = (x_ref[:, cols].astype(F32) * wide[0:128]).astype(BF)
        xw[:, cols] = fed
        gain[:, cols] = wide[128:256]
        dexp[:, cols] = wide[256:264]
        sexp[:, cols] = wide[264:272]
        end = jnp.dot(pt_hi, fed, preferred_element_type=F32) + jnp.dot(
            pt_lo, fed, preferred_element_type=F32
        )
        ends[:, cols] = end[0:STATE]
        return 0

    widen(0, 0)
    widen(1, 0)
    my_half = pl.ds(pl.multiple_of(c * HCH, HCH), HCH)
    sib_half = pl.ds(pl.multiple_of((1 - c) * HCH, HCH), HCH)
    def e_copy():
        return pltpu.make_async_remote_copy(
            src_ref=e_out, dst_ref=e_in, send_sem=esend.at[0], recv_sem=erecv.at[0],
            device_id=(sib, ex), device_id_type=MESH,
        )

    def d_copy():
        return pltpu.make_async_remote_copy(
            src_ref=dexp.at[:, sib_half], dst_ref=d_in, send_sem=esend.at[1],
            recv_sem=erecv.at[1], device_id=(sib, ex), device_id_type=MESH,
        )

    def share_ends():
        e_out[...] = ends[:, sib_half].astype(BF)
        e_copy().start()
        d_copy().start()

    others = pl.ds(0, (NEX - 1) * 16)

    def ids_y():
        return pltpu.make_async_remote_copy(
            src_ref=reqs.at[pl.ds(0, SIDE - 1)], dst_ref=middle_ids.at[pl.ds(0, SIDE - 1)],
            send_sem=isend.at[0], recv_sem=irecv.at[0],
            device_id=(sib, ex), device_id_type=MESH,
        )

    def ids_x():
        part = pl.ds(0, 16 * (SIDE - 1))
        return pltpu.make_async_remote_copy(
            src_ref=middle_ids.at[:, part], dst_ref=ids.at[:, part],
            send_sem=isend.at[1], recv_sem=irecv.at[1],
            device_id=(sib, ex), device_id_type=MESH,
        )

    def blocks_all():
        return pltpu.make_async_remote_copy(
            src_ref=picked.at[others], dst_ref=arrived.at[others],
            send_sem=bsend.at[0], recv_sem=brecv.at[0],
            device_id=(sib, ex), device_id_type=MESH,
        )

    ids_y().wait_recv()

    def ask_x(k, _):
        to = along_x(k)
        part = pl.ds(pl.multiple_of(lax.rem(to, SIDE) * 16, 16), 16)
        pltpu.make_async_remote_copy(
            src_ref=middle_ids.at[:, part], dst_ref=ids.at[:, mine_x],
            send_sem=isend.at[1], recv_sem=irecv.at[1],
            device_id=(me, to), device_id_type=MESH,
        ).start()
        return 0

    lax.fori_loop(1, SIDE, ask_x, 0)
    ids[:, mine_x] = middle_ids[:, mine_x]
    q_load.wait()
    for g in range(KVH):
        for j in range(GRP):
            h = g * GRP + j
            qs[g, j * TOK:(j + 1) * TOK, :] = q_ref[:, h * DIM:(h + 1) * DIM]
    peak[...] = jnp.full_like(peak, LOW)
    acc[...] = jnp.zeros_like(acc)
    def hand_out():
        ids_x().wait_recv()
        got = ids[...].reshape(256, 128)
        same = lax.rem(row, 8) == lax.rem(lane, 8)
        pick = jnp.concatenate(
            [
                ((got == lane // 8) & same).astype(BF),
                ((got == lane // 8 + 16) & same).astype(BF),
            ],
            axis=1,
        )
        pool_load.wait()
        picked[...] = jnp.dot(pick, pool_ref[...], preferred_element_type=F32).astype(BF)
        arrived[mine] = picked[mine]

    def block_copy(k):
        to = lax.rem(ex + k, NEX)
        return pltpu.make_async_remote_copy(
            src_ref=picked.at[pl.ds(pl.multiple_of(to * 16, 16), 16)],
            dst_ref=arrived.at[pl.ds(pl.multiple_of(ex * 16, 16), 16)],
            send_sem=bsend.at[0], recv_sem=brecv.at[0],
            device_id=(me, to), device_id_type=MESH,
        )

    def give(k, _):
        block_copy(k).start()
        return 0

    length = len_ref[ex]

    def attend(start, shown, bias, heads):
        keep = iota((UNIT, DIM), 0) < shown
        one = keep.astype(F32).astype(BF)
        for g in heads:
            kcols = slice(g * DIM, (g + 1) * DIM)
            vcols = slice(512 + g * DIM, 512 + (g + 1) * DIM)
            key = buf[pl.ds(start, UNIT), kcols]
            value = buf[pl.ds(start, UNIT), vcols]
            key = jnp.where(keep, key, jnp.broadcast_to(kv_ref[0:1, kcols], (UNIT, DIM)))
            value = value * one
            score = lax.dot_general(
                qs[g], key, (((1,), (1,)), ((), ())), preferred_element_type=F32
            )
            if bias is not None:
                score = score + bias
            old = peak[g]
            new = jnp.maximum(old, jnp.max(score, axis=1, keepdims=True))
            weight = jnp.exp2((score - jnp.concatenate([new, new], 1)) * SCALE).astype(BF)
            factor = jnp.exp2((old - new) * SCALE)
            acc[g] = acc[g] * jnp.concatenate([factor, factor], 1) + jnp.dot(
                weight, jnp.concatenate([value, one], axis=1), preferred_element_type=F32
            )
            peak[g] = new

    def sib_wait(array, kind, s, half):
        if kind == 0:
            origin = right_origin(s)
        else:
            origin = left_origin(s)
        kv_copy(array, 2 + kind, s, half, origin + 1 - c, sib).wait_recv()

    def own_keys():
        for half in range(2):
            kv_copy(0, 2, 0, half, sib, sib).wait_recv()
        token = lax.rem(iota((GRP * TOK, UNIT), 0), TOK) + c * TOK
        bias = jnp.where(iota((GRP * TOK, UNIT), 1) <= token, 0.0, LOW)
        attend(pl.multiple_of(z * UNIT, UNIT), UNIT, bias, range(KVH))

    def p_copy(k):
        return pltpu.make_async_remote_copy(
            src_ref=p_out.at[k], dst_ref=p_in.at[k], send_sem=psend.at[k],
            recv_sem=precv.at[k], device_id=(right, ex), device_id_type=MESH,
        )

    def c_copy(k):
        return pltpu.make_async_remote_copy(
            src_ref=c_sib.at[k], dst_ref=c_in.at[k], send_sem=csend.at[k],
            recv_sem=crecv.at[k], device_id=(sib, ex), device_id_type=MESH,
        )

    def seed():
        init_load.wait()
        keep = lax.rem(iota((STATE, 2048), 1), STATE) == iota((STATE, 2048), 0)
        deep = iota((2048, 128), 0)
        move = (iota((2048, 128), 1) == lax.rem(deep, 1024) // STATE + 64 * (deep // 1024)).astype(BF)

        def batch(b, _):
            head = pl.multiple_of(c * 64 + b * 16, 16)
            heads = init_ref[pl.ds(head, 16), :]
            parts = []
            for i in range(8):
                pair = jnp.concatenate([heads[2 * i:2 * i + 1], heads[2 * i + 1:2 * i + 2]], axis=1)
                parts.append(jnp.where(keep, jnp.broadcast_to(pair, (STATE, 2048)), 0.0))
            full = jnp.concatenate(parts, axis=0)
            high = full.astype(BF)
            low = (full - high.astype(F32)).astype(BF)
            moved = jnp.dot(high, move, preferred_element_type=F32) + jnp.dot(
                low, move, preferred_element_type=F32
            )
            for i in range(8):
                carried[:, pl.ds(pl.multiple_of(head * 64 + i * 128, 128), 128)] = (
                    moved[i * STATE:(i + 1) * STATE]
                )
            return 0

        lax.fori_loop(0, 4, batch, 0)

    def chain():
        e_copy().wait_recv()
        d_copy().wait_recv()
        for k in range(NSUB):
            cols = pl.ds(pl.multiple_of(c * HCH + k * SUB, SUB), SUB)
            piece = slice(k * SUB, (k + 1) * SUB)

            @pl.when(z > 0)
            def _():
                p_copy(k).wait_recv()
                carried[:, cols] = p_in[k].astype(F32)

            @pl.when(z == 0)
            def _():
                if k == 0:
                    seed()

            entering = carried[:, cols]
            own_e, own_d = ends[:, cols], dexp[0:1, cols]
            sib_e, sib_d = e_in[:, piece].astype(F32), d_in[0:1, piece]
            even = c == 0
            e0, e1 = jnp.where(even, own_e, sib_e), jnp.where(even, sib_e, own_e)
            d0, d1 = jnp.where(even, own_d, sib_d), jnp.where(even, sib_d, own_d)
            middle = d0 * entering + e0
            p_out[k] = (d1 * middle + e1).astype(BF)

            @pl.when(z < NZ - 1)
            def _():
                p_copy(k).start()

            c_sib[k] = jnp.where(even, middle, entering).astype(BF)
            c_copy(k).start()
            carried[:, cols] = jnp.where(even, entering, middle)

    def ssm_ready():
        for k in range(NSUB):
            c_copy(k).wait_recv()
            cols = pl.ds(pl.multiple_of((1 - c) * HCH + k * SUB, SUB), SUB)
            carried[:, cols] = c_in[k].astype(F32)

    def ssm_finish(n):
        cols = pl.ds(pl.multiple_of(n * WIDE, WIDE), WIDE)
        state = (carried[:, cols] * dexp[0:1, cols]).astype(BF)
        state = jnp.concatenate([jnp.zeros((STATE, WIDE), BF), state], axis=0)
        mixed = (
            jnp.dot(amat[...], xw[:, cols], preferred_element_type=F32)
            + jnp.dot(plo[0], state, preferred_element_type=F32)
            + jnp.dot(plo[1], state, preferred_element_type=F32)
        )
        ssm_ref[:, cols] = (
            gain[:, cols] * mixed + sexp[0:1, cols] * x_ref[:, cols].astype(F32)
        ).astype(BF)

    def assemble():
        blocks_all().wait_recv()
        context = jnp.dot(compact[...], arrived[...], preferred_element_type=F32).astype(BF)
        buf[where_rows(1, me, 0)] = context[0:HALF]
        buf[where_rows(1, me, 1)] = context[HALF:TOK]
        send_own(1)

    def stage(k):
        is_ctx = (k == 3) | (k >= 5)
        s = jnp.where(k < 3, k + 1, jnp.where(k == 3, 1, jnp.where(k == 4, 4, k - 3)))
        return jnp.where(is_ctx, 1, 0), s

    turn = 8 + (18 * z) // 7

    def step(fine, _):
        it = fine // 2
        kind = lax.rem(fine, 2)
        early = kind == 0
        k = it // 2
        j = lax.rem(it, 2)
        array, s = stage(k)
        last = 4 - j

        @pl.when(fine == READY)
        def _():
            assemble()

        @pl.when(s <= last)
        def _():
            half = jnp.where(early, j, 1 - j)
            origin = jnp.where(early, right_origin(s), left_origin(s)) + c
            kv_copy(array, kind, s, half, origin, sib).wait_recv()

            @pl.when(s < last)
            def _():
                kv_copy(array, kind, s + 1, half, origin, jnp.where(early, right, left)).start()

            kv_copy(array, 2 + kind, s, half, origin, sib).start()

        @pl.when(fine == 1)
        def _():
            hand_out()

        @pl.when((fine >= 1) & (fine <= 3))
        def _():
            lax.fori_loop(5 * fine - 4, 5 * fine + 1, give, 0)

        @pl.when((fine <= 6) & (fine != 1))
        def _():
            widen(jnp.where(fine == 0, 2, fine + 1), 0)

        @pl.when(fine == 6)
        def _():
            share_ends()

        @pl.when(fine == 7)
        def _():
            own_keys()

        @pl.when(fine == turn)
        def _():
            chain()

        @pl.when(fine == turn + 3)
        def _():
            ssm_ready()

        @pl.when((fine >= turn + 3) & (fine < turn + 3 + CH // WIDE))
        def _():
            ssm_finish(fine - turn - 3)

        parray, ps = stage(k - 1)
        own = (k - 1 == 4) & (j == 1)
        uarray = jnp.where(own, 1, parray)
        chip = jnp.where(
            own, z, lax.rem(jnp.where(j == 0, z + NZ - ps, z + ps), NZ)
        )

        @pl.when(it >= 2)
        def _():
            @pl.when(own & early)
            def _():
                for half in range(2):
                    kv_copy(1, 2, 0, half, sib, sib).wait_recv()

            @pl.when(jnp.logical_not(own) & (ps < 4) & early)
            def _():
                for half in range(2):
                    kv_copy(
                        parray, 2 + j, ps, half,
                        jnp.where(j == 0, right_origin(ps), left_origin(ps)) + 1 - c, sib,
                    ).wait_recv()

            @pl.when(jnp.logical_not(own) & (ps == 4) & early)
            def _():
                sib_wait(parray, 0, 4, 0)
                sib_wait(parray, 1, 4, 1)

            for part in range(2):

                @pl.when(((uarray == 1) | (chip < z)) & (kind == part))
                def _():
                    attend(
                        pl.multiple_of(uarray * 2048 + chip * UNIT, UNIT),
                        jnp.where(uarray == 1, length - chip * UNIT, UNIT),
                        None,
                        (2 * part, 2 * part + 1),
                    )

        return 0

    lax.fori_loop(0, 32, step, 0)

    def rest(n, _):
        ssm_finish(n)
        return 0

    lax.fori_loop(jnp.minimum(CH // WIDE, 32 - turn - 3), CH // WIDE, rest, 0)
    ssm_store.start()
    sib_wait(1, 0, 4, 0)
    sib_wait(1, 1, 4, 1)
    final = lax.rem(z + 4, NZ)
    attend(pl.multiple_of(2048 + final * UNIT, UNIT), length - final * UNIT, None, range(KVH))
    for g in range(KVH):
        sums = acc[g]
        done = (sums[:, 0:DIM] / sums[:, DIM:2 * DIM]).astype(BF)
        for j in range(GRP):
            h = g * GRP + j
            att_ref[:, h * DIM:(h + 1) * DIM] = done[j * TOK:(j + 1) * TOK]

    att_store.start()

    sent = buf.at[pl.ds(0, 60 * HALF)]
    pltpu.make_async_remote_copy(
        src_ref=sent, dst_ref=sent, send_sem=ksend.at[0], recv_sem=krecv.at[0],
        device_id=(sib, ex), device_id_type=MESH,
    ).wait_send()
    ids_y().wait_send()
    ids_x().wait_send()
    blocks_all().wait_send()
    e_copy().wait_send()
    d_copy().wait_send()
    ssm_store.wait()
    att_store.wait()
    for k in range(NSUB):
        c_copy(k).wait_send()

        @pl.when(z < NZ - 1)
        def _():
            p_copy(k).wait_send()


def local(
    queries, new_kv, kv_pool, holders, slots, lengths,
    ssm_input, step_sizes, projections, decay_rates, skip_gain, init_state,
):
    kv = new_kv[0].reshape(TOK, 1024)
    pool = kv_pool.reshape(256, 1024)
    vmem = pl.BlockSpec(memory_space=pltpu.VMEM)
    far = pl.BlockSpec(memory_space=pl.ANY)
    smem = pl.BlockSpec(memory_space=pltpu.SMEM)
    dma = pltpu.SemaphoreType.DMA
    attended, ssm_out = pl.pallas_call(
        kernel,
        out_shape=(
            jax.ShapeDtypeStruct((TOK, 4096), BF),
            jax.ShapeDtypeStruct((TOK, CH), BF),
        ),
        in_specs=[far, vmem, far, vmem, vmem, smem, far] + [vmem] * 4 + [far],
        out_specs=(far, far),
        scratch_shapes=[
            pltpu.VMEM((TOK, 4096), BF),
            pltpu.VMEM((256, 1024), BF),
            pltpu.VMEM((TOK, CH), BF),
            pltpu.VMEM((128, 1024), F32),
            pltpu.VMEM((TOK, 4096), BF),
            pltpu.VMEM((TOK, CH), BF),
            pltpu.VMEM((32 * TOK, 1024), BF),
            pltpu.VMEM((KVH, GRP * TOK, DIM), BF),
            pltpu.VMEM((KVH, GRP * TOK, DIM), F32),
            pltpu.VMEM((KVH, GRP * TOK, 2 * DIM), F32),
            pltpu.VMEM((SIDE, 64, 128), I32),
            pltpu.VMEM((SIDE, 64, 128), I32),
            pltpu.VMEM((SIDE, 64, 128), I32),
            pltpu.VMEM((256, 1024), BF),
            pltpu.VMEM((256, 1024), BF),
            pltpu.VMEM((128, 256), BF),
            pltpu.VMEM((TOK, CH), BF),
            pltpu.VMEM((TOK, CH), F32),
            pltpu.VMEM((8, CH), F32),
            pltpu.VMEM((8, CH), F32),
            pltpu.VMEM((STATE, CH), F32),
            pltpu.VMEM((128, 128), BF),
            pltpu.VMEM((2, 128, 32), BF),
            pltpu.VMEM((STATE, HCH), BF),
            pltpu.VMEM((STATE, HCH), BF),
            pltpu.VMEM((8, HCH), F32),
            pltpu.VMEM((NSUB, STATE, SUB), BF),
            pltpu.VMEM((NSUB, STATE, SUB), BF),
            pltpu.VMEM((NSUB, STATE, SUB), BF),
            pltpu.VMEM((NSUB, STATE, SUB), BF),
            pltpu.VMEM((STATE, CH), F32),
            dma((1,)), dma((80,)),
            dma((2,)), dma((2,)),
            dma((1,)), dma((1,)),
            dma((2,)), dma((2,)),
            dma((NSUB,)), dma((NSUB,)),
            dma((NSUB,)), dma((NSUB,)),
            dma((6,)),
        ],
        compiler_params=pltpu.CompilerParams(
            vmem_limit_bytes=58 * 2 ** 20, collective_id=3, has_side_effects=True
        ),
        name="resume",
    )(
        queries[0], kv, pool, holders, slots, lengths,
        ssm_input[0], step_sizes[0], projections[0].T,
        decay_rates[None], skip_gain[None], init_state[0],
    )
    return attended[None], ssm_out[None]


def solution(mesh):
    placed = (
        P("expert", "seq", None),
        P("expert", "seq", None, None),
        P(("seq", "expert"), None, None, None),
        P("expert", "seq"),
        P("expert", "seq"),
        P(),
        P("expert", "seq", None),
        P("expert", "seq", None),
        P("expert", "seq", None),
        P(),
        P(),
        P("expert", None, None),
    )
    return jax.shard_map(
        local,
        mesh=mesh,
        in_specs=placed,
        out_specs=(P("expert", "seq", None), P("expert", "seq", None)),
        check_vma=False,
    )
```

```python
import functools

import jax
import jax.numpy as jnp
from jax import lax
from jax.experimental import pallas as pl
from jax.experimental.pallas import tpu as pltpu
from jax.sharding import PartitionSpec as P

MESH = pl.DeviceIdType.MESH
BF = jnp.bfloat16
F32 = jnp.float32
I32 = jnp.int32
HIGH = lax.Precision.HIGHEST

KVH = 4
GRP = 8
DIM = 128
TOK = 128
NZ = 8
NEX = 16
READY = 9
SIDE = 4
UNIT = 256
HALF = 64
STATE = 16
CH = 8192
HCH = CH // 2
WIDE = 1024
NSUB = 2
SUB = HCH // NSUB
SCALE = (DIM ** -0.5) * 1.4426950408889634
LOW = -1e30


def iota(shape, axis):
    return lax.broadcasted_iota(I32, shape, axis)


def kernel(
    q_hbm, kv_both, pool_hbm, hold_ref, slot_ref, len_ref,
    x_hbm, step_ref, proj_ref, decay_ref, skip_ref, init_hbm,
    att_hbm, ssm_hbm,
    q_ref, pool_both, kv_ref, pool_ref, x_ref, init_ref, att_ref, ssm_ref,
    buf, qs, peak, acc, reqs, middle_ids, ids, picked, arrived, compact,
    xw, gain, dexp, sexp, ends, amat, plo,
    e_out, e_in, d_in, p_in, p_out, c_sib, c_in, carried,
    ksend, krecv, isend, irecv, bsend, brecv, esend, erecv, psend, precv, csend, crecv, lsend,
):
    me = lax.axis_index("seq")
    ex = lax.axis_index("expert")
    z = me // 2
    c = lax.rem(me, 2)
    right = lax.rem(z + 1, NZ) * 2 + c
    left = lax.rem(z + NZ - 1, NZ) * 2 + c
    sib = z * 2 + 1 - c

    barrier = pltpu.get_barrier_semaphore()
    for d in (right, left, sib):
        pl.semaphore_signal(barrier, inc=1, device_id=(d, ex), device_id_type=MESH)

    ey, exx = ex // SIDE, lax.rem(ex, SIDE)

    def along_y(k):
        return lax.rem(ex + SIDE * k, NEX)

    def along_x(k):
        return ey * SIDE + lax.rem(exx + k, SIDE)

    def greet(k, _):
        pl.semaphore_signal(
            barrier, inc=1, device_id=(me, along_y(k)), device_id_type=MESH
        )
        pl.semaphore_signal(
            barrier, inc=1, device_id=(me, along_x(k)), device_id_type=MESH
        )
        return 0

    lax.fori_loop(1, SIDE, greet, 0)

    x_load = pltpu.make_async_copy(x_hbm, x_ref, lsend.at[0])
    q_load = pltpu.make_async_copy(q_hbm, q_ref, lsend.at[1])
    pool_load = pltpu.make_async_copy(pool_hbm, pool_both, lsend.at[2])
    init_load = pltpu.make_async_copy(init_hbm, init_ref, lsend.at[3])
    att_store = pltpu.make_async_copy(att_ref, att_hbm, lsend.at[4])
    ssm_store = pltpu.make_async_copy(ssm_ref, ssm_hbm, lsend.at[5])
    x_load.start()
    pool_load.start()
    q_load.start()

    @pl.when(z == 0)
    def _():
        init_load.start()

    def where_rows(array, origin, half):
        return pl.ds(pl.multiple_of((array * 16 + origin) * TOK + half * HALF, HALF), HALF)

    def kv_copy(array, kind, s, half, origin, to):
        k = ((array * 4 + kind) * 5 + s) * 2 + half
        ref = buf.at[where_rows(array, origin, half)]
        return pltpu.make_async_remote_copy(
            src_ref=ref, dst_ref=ref, send_sem=ksend.at[0], recv_sem=krecv.at[k],
            device_id=(to, ex), device_id_type=MESH,
        )

    def right_origin(s):
        return lax.rem(z + NZ - s, NZ) * 2

    def left_origin(s):
        return lax.rem(z + s, NZ) * 2

    def send_own(array):
        for half in range(2):
            kv_copy(array, 0, 1, half, me, right).start()
            kv_copy(array, 1, 1, half, me, left).start()
        for half in range(2):
            kv_copy(array, 2, 0, half, me, sib).start()

    kv_ref[:, 0:512] = kv_both[:, 0, :]
    kv_ref[:, 512:1024] = kv_both[:, 1, :]
    buf[where_rows(0, me, 0)] = kv_ref[0:HALF]
    buf[where_rows(0, me, 1)] = kv_ref[HALF:TOK]

    spread = (iota((16, 128), 1) // 8 == iota((16, 128), 0)).astype(F32)
    hold = jnp.dot(hold_ref[...].astype(F32), spread, preferred_element_type=F32)
    slot = jnp.dot(slot_ref[...].astype(F32), spread, preferred_element_type=F32)
    row = iota((256, 128), 0)
    lane = iota((256, 128), 1)
    named = (hold[0:1] == (row // 16).astype(F32)).astype(F32)
    lead = ((iota((128, 128), 0) // 8 < iota((128, 128), 1) // 8)
            & (lax.rem(iota((128, 128), 0), 8) == 0)).astype(BF)
    before = jnp.dot(named.astype(BF), lead, preferred_element_type=F32)
    chosen = named * (before == lax.rem(row // 8, 2).astype(F32)).astype(F32)
    first = (lax.rem(lane, 8) == 0).astype(F32)
    wanted = jnp.sum(chosen * first * slot[0:1], axis=1, keepdims=True)
    reqs[...] = jnp.broadcast_to(wanted, (256, 128)).astype(I32).reshape(SIDE, 64, 128)
    place = chosen * (lax.rem(row, 8) == lax.rem(lane, 8)).astype(F32)
    compact[...] = place.T.astype(BF)

    pl.semaphore_wait(barrier, 9)
    send_own(0)


    def ask_y(k, _):
        to = along_y(k)
        pltpu.make_async_remote_copy(
            src_ref=reqs.at[to // SIDE], dst_ref=middle_ids.at[ey],
            send_sem=isend.at[0], recv_sem=irecv.at[0],
            device_id=(me, to), device_id_type=MESH,
        ).start()
        return 0

    lax.fori_loop(1, SIDE, ask_y, 0)
    middle_ids[ey] = reqs[ey]
    mine_x = pl.ds(pl.multiple_of(exx * 16, 16), 16)
    mine = pl.ds(pl.multiple_of(ex * 16, 16), 16)

    dec = decay_ref[...]
    steps = step_ref[...]
    lower = iota((128, 128), 0) >= iota((128, 128), 1)
    logs = jnp.dot(lower.astype(F32), -steps * dec, precision=HIGH, preferred_element_type=F32)
    total = logs[127:128]
    rows = jnp.concatenate(
        [
            jnp.exp(total - logs) * steps,
            jnp.exp(logs - total),
            jnp.broadcast_to(jnp.exp(total), (8, 128)),
            jnp.broadcast_to(skip_ref[...], (8, 128)),
        ],
        axis=0,
    )
    rows_hi = rows.astype(BF)
    rows_cat = jnp.concatenate([rows_hi, (rows - rows_hi.astype(F32)).astype(BF)], axis=1)
    proj_t = proj_ref[...]
    proj = proj_t.T
    write_t = jnp.concatenate([jnp.zeros((STATE, 128), F32), proj_t[0:STATE]], axis=0)
    affinity = jnp.dot(proj, write_t, precision=HIGH, preferred_element_type=F32)
    amat[...] = jnp.where(lower, affinity, 0.0).astype(BF)
    plo[0] = proj.astype(BF)
    plo[1] = (proj - proj.astype(BF).astype(F32)).astype(BF)
    pt_hi = proj_t.astype(BF)
    pt_lo = (proj_t - pt_hi.astype(F32)).astype(BF)

    x_load.wait()

    def widen(n, _):
        cols = pl.ds(pl.multiple_of(n * WIDE, WIDE), WIDE)
        one = (iota((128, WIDE), 0) == n * (WIDE // 64) + iota((128, WIDE), 1) // 64)
        one = one.astype(BF)
        wide = jnp.dot(
            rows_cat, jnp.concatenate([one, one], axis=0), preferred_element_type=F32
        )
        fed = (x_ref[:, cols].astype(F32) * wide[0:128]).astype(BF)
        xw[:, cols] = fed
        gain[:, cols] = wide[128:256]
        dexp[:, cols] = wide[256:264]
        sexp[:, cols] = wide[264:272]
        end = jnp.dot(pt_hi, fed, preferred_element_type=F32) + jnp.dot(
            pt_lo, fed, preferred_element_type=F32
        )
        ends[:, cols] = end[0:STATE]
        return 0

    widen(0, 0)
    widen(1, 0)
    my_half = pl.ds(pl.multiple_of(c * HCH, HCH), HCH)
    sib_half = pl.ds(pl.multiple_of((1 - c) * HCH, HCH), HCH)
    def e_copy():
        return pltpu.make_async_remote_copy(
            src_ref=e_out, dst_ref=e_in, send_sem=esend.at[0], recv_sem=erecv.at[0],
            device_id=(sib, ex), device_id_type=MESH,
        )

    def d_copy():
        return pltpu.make_async_remote_copy(
            src_ref=dexp.at[:, sib_half], dst_ref=d_in, send_sem=esend.at[1],
            recv_sem=erecv.at[1], device_id=(sib, ex), device_id_type=MESH,
        )

    def share_ends():
        e_out[...] = ends[:, sib_half].astype(BF)
        e_copy().start()
        d_copy().start()

    others = pl.ds(0, (NEX - 1) * 16)

    def ids_y():
        return pltpu.make_async_remote_copy(
            src_ref=reqs.at[pl.ds(0, SIDE - 1)], dst_ref=middle_ids.at[pl.ds(0, SIDE - 1)],
            send_sem=isend.at[0], recv_sem=irecv.at[0],
            device_id=(sib, ex), device_id_type=MESH,
        )

    def ids_x():
        part = pl.ds(0, 16 * (SIDE - 1))
        return pltpu.make_async_remote_copy(
            src_ref=middle_ids.at[:, part], dst_ref=ids.at[:, part],
            send_sem=isend.at[1], recv_sem=irecv.at[1],
            device_id=(sib, ex), device_id_type=MESH,
        )

    def blocks_all():
        return pltpu.make_async_remote_copy(
            src_ref=picked.at[others], dst_ref=arrived.at[others],
            send_sem=bsend.at[0], recv_sem=brecv.at[0],
            device_id=(sib, ex), device_id_type=MESH,
        )

    ids_y().wait_recv()

    def ask_x(k, _):
        to = along_x(k)
        part = pl.ds(pl.multiple_of(lax.rem(to, SIDE) * 16, 16), 16)
        pltpu.make_async_remote_copy(
            src_ref=middle_ids.at[:, part], dst_ref=ids.at[:, mine_x],
            send_sem=isend.at[1], recv_sem=irecv.at[1],
            device_id=(me, to), device_id_type=MESH,
        ).start()
        return 0

    lax.fori_loop(1, SIDE, ask_x, 0)
    ids[:, mine_x] = middle_ids[:, mine_x]
    q_load.wait()
    for g in range(KVH):
        for j in range(GRP):
            h = g * GRP + j
            qs[g, j * TOK:(j + 1) * TOK, :] = q_ref[:, h * DIM:(h + 1) * DIM]
    peak[...] = jnp.full_like(peak, LOW)
    acc[...] = jnp.zeros_like(acc)
    def hand_out():
        ids_x().wait_recv()
        got = ids[...].reshape(256, 128)
        same = lax.rem(row, 8) == lax.rem(lane, 8)
        pick = jnp.concatenate(
            [
                ((got == lane // 8) & same).astype(BF),
                ((got == lane // 8 + 16) & same).astype(BF),
            ],
            axis=1,
        )
        pool_load.wait()
        pool_ref[:, 0:512] = pool_both[:, 0, :]
        pool_ref[:, 512:1024] = pool_both[:, 1, :]
        picked[...] = jnp.dot(pick, pool_ref[...], preferred_element_type=F32).astype(BF)
        arrived[mine] = picked[mine]

    def block_copy(k):
        to = lax.rem(ex + k, NEX)
        return pltpu.make_async_remote_copy(
            src_ref=picked.at[pl.ds(pl.multiple_of(to * 16, 16), 16)],
            dst_ref=arrived.at[pl.ds(pl.multiple_of(ex * 16, 16), 16)],
            send_sem=bsend.at[0], recv_sem=brecv.at[0],
            device_id=(me, to), device_id_type=MESH,
        )

    def give(k, _):
        block_copy(k).start()
        return 0

    length = len_ref[ex]

    def attend(start, shown, bias, heads):
        keep = iota((UNIT, DIM), 0) < shown
        one = keep.astype(F32).astype(BF)
        for g in heads:
            kcols = slice(g * DIM, (g + 1) * DIM)
            vcols = slice(512 + g * DIM, 512 + (g + 1) * DIM)
            key = buf[pl.ds(start, UNIT), kcols]
            value = buf[pl.ds(start, UNIT), vcols]
            key = jnp.where(keep, key, jnp.broadcast_to(kv_ref[0:1, kcols], (UNIT, DIM)))
            value = value * one
            score = lax.dot_general(
                qs[g], key, (((1,), (1,)), ((), ())), preferred_element_type=F32
            )
            if bias is not None:
                score = score + bias
            old = peak[g]
            new = jnp.maximum(old, jnp.max(score, axis=1, keepdims=True))
            weight = jnp.exp2((score - jnp.concatenate([new, new], 1)) * SCALE).astype(BF)
            factor = jnp.exp2((old - new) * SCALE)
            acc[g] = acc[g] * jnp.concatenate([factor, factor], 1) + jnp.dot(
                weight, jnp.concatenate([value, one], axis=1), preferred_element_type=F32
            )
            peak[g] = new

    def sib_wait(array, kind, s, half):
        if kind == 0:
            origin = right_origin(s)
        else:
            origin = left_origin(s)
        kv_copy(array, 2 + kind, s, half, origin + 1 - c, sib).wait_recv()

    def own_keys():
        for half in range(2):
            kv_copy(0, 2, 0, half, sib, sib).wait_recv()
        token = lax.rem(iota((GRP * TOK, UNIT), 0), TOK) + c * TOK
        bias = jnp.where(iota((GRP * TOK, UNIT), 1) <= token, 0.0, LOW)
        attend(pl.multiple_of(z * UNIT, UNIT), UNIT, bias, range(KVH))

    def p_copy(k):
        return pltpu.make_async_remote_copy(
            src_ref=p_out.at[k], dst_ref=p_in.at[k], send_sem=psend.at[k],
            recv_sem=precv.at[k], device_id=(right, ex), device_id_type=MESH,
        )

    def c_copy(k):
        return pltpu.make_async_remote_copy(
            src_ref=c_sib.at[k], dst_ref=c_in.at[k], send_sem=csend.at[k],
            recv_sem=crecv.at[k], device_id=(sib, ex), device_id_type=MESH,
        )

    def seed():
        init_load.wait()
        keep = lax.rem(iota((STATE, 2048), 1), STATE) == iota((STATE, 2048), 0)
        deep = iota((2048, 128), 0)
        move = (iota((2048, 128), 1) == lax.rem(deep, 1024) // STATE + 64 * (deep // 1024)).astype(BF)

        def batch(b, _):
            head = pl.multiple_of(c * 64 + b * 16, 16)
            heads = init_ref[pl.ds(head, 16), :]
            parts = []
            for i in range(8):
                pair = jnp.concatenate([heads[2 * i:2 * i + 1], heads[2 * i + 1:2 * i + 2]], axis=1)
                parts.append(jnp.where(keep, jnp.broadcast_to(pair, (STATE, 2048)), 0.0))
            full = jnp.concatenate(parts, axis=0)
            high = full.astype(BF)
            low = (full - high.astype(F32)).astype(BF)
            moved = jnp.dot(high, move, preferred_element_type=F32) + jnp.dot(
                low, move, preferred_element_type=F32
            )
            for i in range(8):
                carried[:, pl.ds(pl.multiple_of(head * 64 + i * 128, 128), 128)] = (
                    moved[i * STATE:(i + 1) * STATE]
                )
            return 0

        lax.fori_loop(0, 4, batch, 0)

    def chain():
        e_copy().wait_recv()
        d_copy().wait_recv()
        for k in range(NSUB):
            cols = pl.ds(pl.multiple_of(c * HCH + k * SUB, SUB), SUB)
            piece = slice(k * SUB, (k + 1) * SUB)

            @pl.when(z > 0)
            def _():
                p_copy(k).wait_recv()
                carried[:, cols] = p_in[k].astype(F32)

            @pl.when(z == 0)
            def _():
                if k == 0:
                    seed()

            entering = carried[:, cols]
            own_e, own_d = ends[:, cols], dexp[0:1, cols]
            sib_e, sib_d = e_in[:, piece].astype(F32), d_in[0:1, piece]
            even = c == 0
            e0, e1 = jnp.where(even, own_e, sib_e), jnp.where(even, sib_e, own_e)
            d0, d1 = jnp.where(even, own_d, sib_d), jnp.where(even, sib_d, own_d)
            middle = d0 * entering + e0
            p_out[k] = (d1 * middle + e1).astype(BF)

            @pl.when(z < NZ - 1)
            def _():
                p_copy(k).start()

            c_sib[k] = jnp.where(even, middle, entering).astype(BF)
            c_copy(k).start()
            carried[:, cols] = jnp.where(even, entering, middle)

    def ssm_ready():
        for k in range(NSUB):
            c_copy(k).wait_recv()
            cols = pl.ds(pl.multiple_of((1 - c) * HCH + k * SUB, SUB), SUB)
            carried[:, cols] = c_in[k].astype(F32)

    def ssm_finish(n):
        cols = pl.ds(pl.multiple_of(n * WIDE, WIDE), WIDE)
        state = (carried[:, cols] * dexp[0:1, cols]).astype(BF)
        state = jnp.concatenate([jnp.zeros((STATE, WIDE), BF), state], axis=0)
        mixed = (
            jnp.dot(amat[...], xw[:, cols], preferred_element_type=F32)
            + jnp.dot(plo[0], state, preferred_element_type=F32)
            + jnp.dot(plo[1], state, preferred_element_type=F32)
        )
        ssm_ref[:, cols] = (
            gain[:, cols] * mixed + sexp[0:1, cols] * x_ref[:, cols].astype(F32)
        ).astype(BF)

    def assemble():
        blocks_all().wait_recv()
        context = jnp.dot(compact[...], arrived[...], preferred_element_type=F32).astype(BF)
        buf[where_rows(1, me, 0)] = context[0:HALF]
        buf[where_rows(1, me, 1)] = context[HALF:TOK]
        send_own(1)

    def stage(k):
        is_ctx = (k == 3) | (k >= 5)
        s = jnp.where(k < 3, k + 1, jnp.where(k == 3, 1, jnp.where(k == 4, 4, k - 3)))
        return jnp.where(is_ctx, 1, 0), s

    turn = 8 + (18 * z) // 7

    def step(fine, _):
        it = fine // 2
        kind = lax.rem(fine, 2)
        early = kind == 0
        k = it // 2
        j = lax.rem(it, 2)
        array, s = stage(k)
        last = 4 - j

        @pl.when(fine == READY)
        def _():
            assemble()

        @pl.when(s <= last)
        def _():
            half = jnp.where(early, j, 1 - j)
            origin = jnp.where(early, right_origin(s), left_origin(s)) + c
            kv_copy(array, kind, s, half, origin, sib).wait_recv()

            @pl.when(s < last)
            def _():
                kv_copy(array, kind, s + 1, half, origin, jnp.where(early, right, left)).start()

            kv_copy(array, 2 + kind, s, half, origin, sib).start()

        @pl.when(fine == 1)
        def _():
            hand_out()

        @pl.when((fine >= 1) & (fine <= 3))
        def _():
            lax.fori_loop(5 * fine - 4, 5 * fine + 1, give, 0)

        @pl.when((fine <= 6) & (fine != 1))
        def _():
            widen(jnp.where(fine == 0, 2, fine + 1), 0)

        @pl.when(fine == 6)
        def _():
            share_ends()

        @pl.when(fine == 7)
        def _():
            own_keys()

        @pl.when(fine == turn)
        def _():
            chain()

        @pl.when(fine == turn + 3)
        def _():
            ssm_ready()

        @pl.when((fine >= turn + 3) & (fine < turn + 3 + CH // WIDE))
        def _():
            ssm_finish(fine - turn - 3)

        parray, ps = stage(k - 1)
        own = (k - 1 == 4) & (j == 1)
        uarray = jnp.where(own, 1, parray)
        chip = jnp.where(
            own, z, lax.rem(jnp.where(j == 0, z + NZ - ps, z + ps), NZ)
        )

        @pl.when(it >= 2)
        def _():
            @pl.when(own & early)
            def _():
                for half in range(2):
                    kv_copy(1, 2, 0, half, sib, sib).wait_recv()

            @pl.when(jnp.logical_not(own) & (ps < 4) & early)
            def _():
                for half in range(2):
                    kv_copy(
                        parray, 2 + j, ps, half,
                        jnp.where(j == 0, right_origin(ps), left_origin(ps)) + 1 - c, sib,
                    ).wait_recv()

            @pl.when(jnp.logical_not(own) & (ps == 4) & early)
            def _():
                sib_wait(parray, 0, 4, 0)
                sib_wait(parray, 1, 4, 1)

            for part in range(2):

                @pl.when(((uarray == 1) | (chip < z)) & (kind == part))
                def _():
                    attend(
                        pl.multiple_of(uarray * 2048 + chip * UNIT, UNIT),
                        jnp.where(uarray == 1, length - chip * UNIT, UNIT),
                        None,
                        (2 * part, 2 * part + 1),
                    )

        return 0

    lax.fori_loop(0, 32, step, 0)

    def rest(n, _):
        ssm_finish(n)
        return 0

    lax.fori_loop(jnp.minimum(CH // WIDE, 32 - turn - 3), CH // WIDE, rest, 0)
    ssm_store.start()
    sib_wait(1, 0, 4, 0)
    sib_wait(1, 1, 4, 1)
    final = lax.rem(z + 4, NZ)
    attend(pl.multiple_of(2048 + final * UNIT, UNIT), length - final * UNIT, None, range(KVH))
    for g in range(KVH):
        sums = acc[g]
        done = (sums[:, 0:DIM] / sums[:, DIM:2 * DIM]).astype(BF)
        for j in range(GRP):
            h = g * GRP + j
            att_ref[:, h * DIM:(h + 1) * DIM] = done[j * TOK:(j + 1) * TOK]

    att_store.start()

    sent = buf.at[pl.ds(0, 60 * HALF)]
    pltpu.make_async_remote_copy(
        src_ref=sent, dst_ref=sent, send_sem=ksend.at[0], recv_sem=krecv.at[0],
        device_id=(sib, ex), device_id_type=MESH,
    ).wait_send()
    ids_y().wait_send()
    ids_x().wait_send()
    blocks_all().wait_send()
    e_copy().wait_send()
    d_copy().wait_send()
    ssm_store.wait()
    att_store.wait()
    for k in range(NSUB):
        c_copy(k).wait_send()

        @pl.when(z < NZ - 1)
        def _():
            p_copy(k).wait_send()


def local(
    queries, new_kv, kv_pool, holders, slots, lengths,
    ssm_input, step_sizes, projections, decay_rates, skip_gain, init_state,
):
    kv = new_kv[0]
    pool = kv_pool.reshape(256, 2, 512)
    vmem = pl.BlockSpec(memory_space=pltpu.VMEM)
    far = pl.BlockSpec(memory_space=pl.ANY)
    smem = pl.BlockSpec(memory_space=pltpu.SMEM)
    dma = pltpu.SemaphoreType.DMA
    attended, ssm_out = pl.pallas_call(
        kernel,
        out_shape=(
            jax.ShapeDtypeStruct((TOK, 4096), BF),
            jax.ShapeDtypeStruct((TOK, CH), BF),
        ),
        in_specs=[far, vmem, far, vmem, vmem, smem, far] + [vmem] * 4 + [far],
        out_specs=(far, far),
        scratch_shapes=[
            pltpu.VMEM((TOK, 4096), BF),
            pltpu.VMEM((256, 2, 512), BF),
            pltpu.VMEM((TOK, 1024), BF),
            pltpu.VMEM((256, 1024), BF),
            pltpu.VMEM((TOK, CH), BF),
            pltpu.VMEM((128, 1024), F32),
            pltpu.VMEM((TOK, 4096), BF),
            pltpu.VMEM((TOK, CH), BF),
            pltpu.VMEM((32 * TOK, 1024), BF),
            pltpu.VMEM((KVH, GRP * TOK, DIM), BF),
            pltpu.VMEM((KVH, GRP * TOK, DIM), F32),
            pltpu.VMEM((KVH, GRP * TOK, 2 * DIM), F32),
            pltpu.VMEM((SIDE, 64, 128), I32),
            pltpu.VMEM((SIDE, 64, 128), I32),
            pltpu.VMEM((SIDE, 64, 128), I32),
            pltpu.VMEM((256, 1024), BF),
            pltpu.VMEM((256, 1024), BF),
            pltpu.VMEM((128, 256), BF),
            pltpu.VMEM((TOK, CH), BF),
            pltpu.VMEM((TOK, CH), F32),
            pltpu.VMEM((8, CH), F32),
            pltpu.VMEM((8, CH), F32),
            pltpu.VMEM((STATE, CH), F32),
            pltpu.VMEM((128, 128), BF),
            pltpu.VMEM((2, 128, 32), BF),
            pltpu.VMEM((STATE, HCH), BF),
            pltpu.VMEM((STATE, HCH), BF),
            pltpu.VMEM((8, HCH), F32),
            pltpu.VMEM((NSUB, STATE, SUB), BF),
            pltpu.VMEM((NSUB, STATE, SUB), BF),
            pltpu.VMEM((NSUB, STATE, SUB), BF),
            pltpu.VMEM((NSUB, STATE, SUB), BF),
            pltpu.VMEM((STATE, CH), F32),
            dma((1,)), dma((80,)),
            dma((2,)), dma((2,)),
            dma((1,)), dma((1,)),
            dma((2,)), dma((2,)),
            dma((NSUB,)), dma((NSUB,)),
            dma((NSUB,)), dma((NSUB,)),
            dma((6,)),
        ],
        compiler_params=pltpu.CompilerParams(
            vmem_limit_bytes=58 * 2 ** 20, collective_id=3, has_side_effects=True
        ),
        name="resume",
    )(
        queries[0], kv, pool, holders, slots, lengths,
        ssm_input[0], step_sizes[0], projections[0].T,
        decay_rates[None], skip_gain[None], init_state[0],
    )
    return attended[None], ssm_out[None]


def solution(mesh):
    placed = (
        P("expert", "seq", None),
        P("expert", "seq", None, None),
        P(("seq", "expert"), None, None, None),
        P("expert", "seq"),
        P("expert", "seq"),
        P(),
        P("expert", "seq", None),
        P("expert", "seq", None),
        P("expert", "seq", None),
        P(),
        P(),
        P("expert", None, None),
    )
    return jax.shard_map(
        local,
        mesh=mesh,
        in_specs=placed,
        out_specs=(P("expert", "seq", None), P("expert", "seq", None)),
        check_vma=False,
    )
```

```python
import functools

import jax
import jax.numpy as jnp
from jax import lax
from jax.experimental import pallas as pl
from jax.experimental.pallas import tpu as pltpu
from jax.sharding import PartitionSpec as P

MESH = pl.DeviceIdType.MESH
BF = jnp.bfloat16
F32 = jnp.float32
I32 = jnp.int32
HIGH = lax.Precision.HIGHEST

KVH = 4
GRP = 8
DIM = 128
TOK = 128
NZ = 8
NEX = 16
READY = 9
SIDE = 4
UNIT = 256
HALF = 64
STATE = 16
CH = 8192
HCH = CH // 2
WIDE = 1024
NSUB = 2
SUB = HCH // NSUB
SCALE = (DIM ** -0.5) * 1.4426950408889634
LOW = -1e30


def iota(shape, axis):
    return lax.broadcasted_iota(I32, shape, axis)


def kernel(
    q_hbm, kv_both, pool_hbm, hold_ref, slot_ref, len_ref,
    x_hbm, step_ref, proj_ref, decay_ref, skip_ref, init_hbm,
    att_hbm, ssm_hbm,
    q_ref, pool_both, kv_ref, pool_ref, x_ref, init_ref, att_ref, ssm_ref,
    buf, qs, peak, acc, reqs, middle_ids, ids, picked, arrived, compact,
    xw, gain, dexp, sexp, ends, amat, plo,
    e_out, e_in, d_in, p_in, p_out, c_sib, c_in, carried,
    ksend, krecv, isend, irecv, bsend, brecv, esend, erecv, psend, precv, csend, crecv, lsend,
):
    me = lax.axis_index("seq")
    ex = lax.axis_index("expert")
    z = me // 2
    c = lax.rem(me, 2)
    right = lax.rem(z + 1, NZ) * 2 + c
    left = lax.rem(z + NZ - 1, NZ) * 2 + c
    sib = z * 2 + 1 - c

    barrier = pltpu.get_barrier_semaphore()
    for d in (right, left, sib):
        pl.semaphore_signal(barrier, inc=1, device_id=(d, ex), device_id_type=MESH)

    ey, exx = ex // SIDE, lax.rem(ex, SIDE)

    def along_y(k):
        return lax.rem(ex + SIDE * k, NEX)

    def along_x(k):
        return ey * SIDE + lax.rem(exx + k, SIDE)

    def greet(k, _):
        pl.semaphore_signal(
            barrier, inc=1, device_id=(me, along_y(k)), device_id_type=MESH
        )
        pl.semaphore_signal(
            barrier, inc=1, device_id=(me, along_x(k)), device_id_type=MESH
        )
        return 0

    lax.fori_loop(1, SIDE, greet, 0)

    x_load = pltpu.make_async_copy(x_hbm, x_ref, lsend.at[0])
    q_load = pltpu.make_async_copy(q_hbm, q_ref, lsend.at[1])
    pool_load = pltpu.make_async_copy(pool_hbm, pool_both, lsend.at[2])
    init_load = pltpu.make_async_copy(init_hbm, init_ref, lsend.at[3])
    att_store = pltpu.make_async_copy(att_ref, att_hbm, lsend.at[4])
    ssm_store = pltpu.make_async_copy(ssm_ref, ssm_hbm, lsend.at[5])
    x_load.start()
    pool_load.start()
    q_load.start()

    @pl.when(z == 0)
    def _():
        init_load.start()

    def where_rows(array, origin, half):
        return pl.ds(pl.multiple_of((array * 16 + origin) * TOK + half * HALF, HALF), HALF)

    def kv_copy(array, kind, s, half, origin, to):
        k = ((array * 4 + kind) * 5 + s) * 2 + half
        ref = buf.at[where_rows(array, origin, half)]
        return pltpu.make_async_remote_copy(
            src_ref=ref, dst_ref=ref, send_sem=ksend.at[0], recv_sem=krecv.at[k],
            device_id=(to, ex), device_id_type=MESH,
        )

    def right_origin(s):
        return lax.rem(z + NZ - s, NZ) * 2

    def left_origin(s):
        return lax.rem(z + s, NZ) * 2

    def send_own(array):
        for half in range(2):
            kv_copy(array, 0, 1, half, me, right).start()
            kv_copy(array, 1, 1, half, me, left).start()
        for half in range(2):
            kv_copy(array, 2, 0, half, me, sib).start()

    kv_ref[:, 0:512] = kv_both[:, 0, :]
    kv_ref[:, 512:1024] = kv_both[:, 1, :]
    buf[where_rows(0, me, 0)] = kv_ref[0:HALF]
    buf[where_rows(0, me, 1)] = kv_ref[HALF:TOK]

    spread = (iota((16, 128), 1) // 8 == iota((16, 128), 0)).astype(F32)
    hold = jnp.dot(hold_ref[...].astype(F32), spread, preferred_element_type=F32)
    slot = jnp.dot(slot_ref[...].astype(F32), spread, preferred_element_type=F32)
    row = iota((256, 128), 0)
    lane = iota((256, 128), 1)
    named = (hold[0:1] == (row // 16).astype(F32)).astype(F32)
    lead = ((iota((128, 128), 0) // 8 < iota((128, 128), 1) // 8)
            & (lax.rem(iota((128, 128), 0), 8) == 0)).astype(BF)
    before = jnp.dot(named.astype(BF), lead, preferred_element_type=F32)
    chosen = named * (before == lax.rem(row // 8, 2).astype(F32)).astype(F32)
    first = (lax.rem(lane, 8) == 0).astype(F32)
    wanted = jnp.sum(chosen * first * slot[0:1], axis=1, keepdims=True)
    reqs[...] = jnp.broadcast_to(wanted, (256, 128)).astype(I32).reshape(SIDE, 64, 128)
    place = chosen * (lax.rem(row, 8) == lax.rem(lane, 8)).astype(F32)
    compact[...] = place.T.astype(BF)

    pl.semaphore_wait(barrier, 9)
    send_own(0)


    def ask_y(k, _):
        to = along_y(k)
        pltpu.make_async_remote_copy(
            src_ref=reqs.at[to // SIDE], dst_ref=middle_ids.at[ey],
            send_sem=isend.at[0], recv_sem=irecv.at[0],
            device_id=(me, to), device_id_type=MESH,
        ).start()
        return 0

    lax.fori_loop(1, SIDE, ask_y, 0)
    middle_ids[ey] = reqs[ey]
    mine_x = pl.ds(pl.multiple_of(exx * 16, 16), 16)
    mine = pl.ds(pl.multiple_of(ex * 16, 16), 16)

    dec = decay_ref[...]
    steps = step_ref[...]
    lower = iota((128, 128), 0) >= iota((128, 128), 1)
    logs = jnp.dot(lower.astype(F32), -steps * dec, precision=HIGH, preferred_element_type=F32)
    total = logs[127:128]
    rows = jnp.concatenate(
        [
            jnp.exp(total - logs) * steps,
            jnp.exp(logs - total),
            jnp.broadcast_to(jnp.exp(total), (8, 128)),
            jnp.broadcast_to(skip_ref[...], (8, 128)),
        ],
        axis=0,
    )
    rows_hi = rows.astype(BF)
    rows_cat = jnp.concatenate([rows_hi, (rows - rows_hi.astype(F32)).astype(BF)], axis=1)
    proj_t = proj_ref[...]
    proj = proj_t.T
    write_t = jnp.concatenate([jnp.zeros((STATE, 128), F32), proj_t[0:STATE]], axis=0)
    affinity = jnp.dot(proj, write_t, precision=HIGH, preferred_element_type=F32)
    amat[...] = jnp.where(lower, affinity, 0.0).astype(BF)
    plo[0] = proj.astype(BF)
    plo[1] = (proj - proj.astype(BF).astype(F32)).astype(BF)
    pt_hi = proj_t.astype(BF)
    pt_lo = (proj_t - pt_hi.astype(F32)).astype(BF)

    x_load.wait()

    def widen(n, _):
        cols = pl.ds(pl.multiple_of(n * WIDE, WIDE), WIDE)
        one = (iota((128, WIDE), 0) == n * (WIDE // 64) + iota((128, WIDE), 1) // 64)
        one = one.astype(BF)
        wide = jnp.dot(
            rows_cat, jnp.concatenate([one, one], axis=0), preferred_element_type=F32
        )
        fed = (x_ref[:, cols].astype(F32) * wide[0:128]).astype(BF)
        xw[:, cols] = fed
        gain[:, cols] = wide[128:256]
        dexp[:, cols] = wide[256:264]
        sexp[:, cols] = wide[264:272]
        end = jnp.dot(pt_hi, fed, preferred_element_type=F32) + jnp.dot(
            pt_lo, fed, preferred_element_type=F32
        )
        ends[:, cols] = end[0:STATE]
        return 0

    widen(0, 0)
    widen(1, 0)
    my_half = pl.ds(pl.multiple_of(c * HCH, HCH), HCH)
    sib_half = pl.ds(pl.multiple_of((1 - c) * HCH, HCH), HCH)
    def e_copy():
        return pltpu.make_async_remote_copy(
            src_ref=e_out, dst_ref=e_in, send_sem=esend.at[0], recv_sem=erecv.at[0],
            device_id=(sib, ex), device_id_type=MESH,
        )

    def d_copy():
        return pltpu.make_async_remote_copy(
            src_ref=dexp.at[:, sib_half], dst_ref=d_in, send_sem=esend.at[1],
            recv_sem=erecv.at[1], device_id=(sib, ex), device_id_type=MESH,
        )

    def share_ends():
        e_out[...] = ends[:, sib_half].astype(BF)
        e_copy().start()
        d_copy().start()

    others = pl.ds(0, (NEX - 1) * 16)

    def ids_y():
        return pltpu.make_async_remote_copy(
            src_ref=reqs.at[pl.ds(0, SIDE - 1)], dst_ref=middle_ids.at[pl.ds(0, SIDE - 1)],
            send_sem=isend.at[0], recv_sem=irecv.at[0],
            device_id=(sib, ex), device_id_type=MESH,
        )

    def ids_x():
        part = pl.ds(0, 16 * (SIDE - 1))
        return pltpu.make_async_remote_copy(
            src_ref=middle_ids.at[:, part], dst_ref=ids.at[:, part],
            send_sem=isend.at[1], recv_sem=irecv.at[1],
            device_id=(sib, ex), device_id_type=MESH,
        )

    def blocks_all():
        return pltpu.make_async_remote_copy(
            src_ref=picked.at[others], dst_ref=arrived.at[others],
            send_sem=bsend.at[0], recv_sem=brecv.at[0],
            device_id=(sib, ex), device_id_type=MESH,
        )

    ids_y().wait_recv()

    def ask_x(k, _):
        to = along_x(k)
        part = pl.ds(pl.multiple_of(lax.rem(to, SIDE) * 16, 16), 16)
        pltpu.make_async_remote_copy(
            src_ref=middle_ids.at[:, part], dst_ref=ids.at[:, mine_x],
            send_sem=isend.at[1], recv_sem=irecv.at[1],
            device_id=(me, to), device_id_type=MESH,
        ).start()
        return 0

    lax.fori_loop(1, SIDE, ask_x, 0)
    ids[:, mine_x] = middle_ids[:, mine_x]
    q_load.wait()
    for g in range(KVH):
        for j in range(GRP):
            h = g * GRP + j
            qs[g, j * TOK:(j + 1) * TOK, :] = q_ref[:, h * DIM:(h + 1) * DIM]
    peak[...] = jnp.full_like(peak, LOW)
    acc[...] = jnp.zeros_like(acc)
    def hand_out():
        ids_x().wait_recv()
        got = ids[...].reshape(256, 128)
        same = lax.rem(row, 8) == lax.rem(lane, 8)
        pick = jnp.concatenate(
            [
                ((got == lane // 8) & same).astype(BF),
                ((got == lane // 8 + 16) & same).astype(BF),
            ],
            axis=1,
        )
        pool_load.wait()
        pool_ref[:, 0:512] = pool_both[:, 0, :]
        pool_ref[:, 512:1024] = pool_both[:, 1, :]
        picked[...] = jnp.dot(pick, pool_ref[...], preferred_element_type=F32).astype(BF)
        arrived[mine] = picked[mine]

    def block_copy(k):
        to = lax.rem(ex + k, NEX)
        return pltpu.make_async_remote_copy(
            src_ref=picked.at[pl.ds(pl.multiple_of(to * 16, 16), 16)],
            dst_ref=arrived.at[pl.ds(pl.multiple_of(ex * 16, 16), 16)],
            send_sem=bsend.at[0], recv_sem=brecv.at[0],
            device_id=(me, to), device_id_type=MESH,
        )

    def give(k, _):
        block_copy(k).start()
        return 0

    length = len_ref[ex]

    def attend(start, shown, bias, heads):
        keep = iota((UNIT, DIM), 0) < shown
        one = keep.astype(F32).astype(BF)
        for g in heads:
            kcols = slice(g * DIM, (g + 1) * DIM)
            vcols = slice(512 + g * DIM, 512 + (g + 1) * DIM)
            key = buf[pl.ds(start, UNIT), kcols]
            value = buf[pl.ds(start, UNIT), vcols]
            key = jnp.where(keep, key, jnp.broadcast_to(kv_ref[0:1, kcols], (UNIT, DIM)))
            value = value * one
            score = lax.dot_general(
                qs[g], key, (((1,), (1,)), ((), ())), preferred_element_type=F32
            )
            if bias is not None:
                score = score + bias
            old = peak[g]
            new = jnp.maximum(old, jnp.max(score, axis=1, keepdims=True))
            weight = jnp.exp2((score - jnp.concatenate([new, new], 1)) * SCALE).astype(BF)
            factor = jnp.exp2((old - new) * SCALE)
            acc[g] = acc[g] * jnp.concatenate([factor, factor], 1) + jnp.dot(
                weight, jnp.concatenate([value, one], axis=1), preferred_element_type=F32
            )
            peak[g] = new

    def sib_wait(array, kind, s, half):
        if kind == 0:
            origin = right_origin(s)
        else:
            origin = left_origin(s)
        kv_copy(array, 2 + kind, s, half, origin + 1 - c, sib).wait_recv()

    def own_keys():
        for half in range(2):
            kv_copy(0, 2, 0, half, sib, sib).wait_recv()
        token = lax.rem(iota((GRP * TOK, UNIT), 0), TOK) + c * TOK
        bias = jnp.where(iota((GRP * TOK, UNIT), 1) <= token, 0.0, LOW)
        attend(pl.multiple_of(z * UNIT, UNIT), UNIT, bias, range(KVH))

    def p_copy(k):
        return pltpu.make_async_remote_copy(
            src_ref=p_out.at[k], dst_ref=p_in.at[k], send_sem=psend.at[k],
            recv_sem=precv.at[k], device_id=(right, ex), device_id_type=MESH,
        )

    def c_copy(k):
        return pltpu.make_async_remote_copy(
            src_ref=c_sib.at[k], dst_ref=c_in.at[k], send_sem=csend.at[k],
            recv_sem=crecv.at[k], device_id=(sib, ex), device_id_type=MESH,
        )

    def seed():
        init_load.wait()
        keep = lax.rem(iota((STATE, 2048), 1), STATE) == iota((STATE, 2048), 0)
        deep = iota((2048, 128), 0)
        move = (iota((2048, 128), 1) == lax.rem(deep, 1024) // STATE + 64 * (deep // 1024)).astype(BF)

        def batch(b, _):
            head = pl.multiple_of(c * 64 + b * 16, 16)
            heads = init_ref[pl.ds(head, 16), :]
            parts = []
            for i in range(8):
                pair = jnp.concatenate([heads[2 * i:2 * i + 1], heads[2 * i + 1:2 * i + 2]], axis=1)
                parts.append(jnp.where(keep, jnp.broadcast_to(pair, (STATE, 2048)), 0.0))
            full = jnp.concatenate(parts, axis=0)
            high = full.astype(BF)
            low = (full - high.astype(F32)).astype(BF)
            moved = jnp.dot(high, move, preferred_element_type=F32) + jnp.dot(
                low, move, preferred_element_type=F32
            )
            for i in range(8):
                carried[:, pl.ds(pl.multiple_of(head * 64 + i * 128, 128), 128)] = (
                    moved[i * STATE:(i + 1) * STATE]
                )
            return 0

        lax.fori_loop(0, 4, batch, 0)

    def chain():
        e_copy().wait_recv()
        d_copy().wait_recv()
        for k in range(NSUB):
            cols = pl.ds(pl.multiple_of(c * HCH + k * SUB, SUB), SUB)
            piece = slice(k * SUB, (k + 1) * SUB)

            @pl.when(z > 0)
            def _():
                p_copy(k).wait_recv()
                carried[:, cols] = p_in[k].astype(F32)

            @pl.when(z == 0)
            def _():
                if k == 0:
                    seed()

            entering = carried[:, cols]
            own_e, own_d = ends[:, cols], dexp[0:1, cols]
            sib_e, sib_d = e_in[:, piece].astype(F32), d_in[0:1, piece]
            even = c == 0
            e0, e1 = jnp.where(even, own_e, sib_e), jnp.where(even, sib_e, own_e)
            d0, d1 = jnp.where(even, own_d, sib_d), jnp.where(even, sib_d, own_d)
            middle = d0 * entering + e0
            p_out[k] = (d1 * middle + e1).astype(BF)

            @pl.when(z < NZ - 1)
            def _():
                p_copy(k).start()

            c_sib[k] = jnp.where(even, middle, entering).astype(BF)
            c_copy(k).start()
            carried[:, cols] = jnp.where(even, entering, middle)

    def ssm_ready():
        for k in range(NSUB):
            c_copy(k).wait_recv()
            cols = pl.ds(pl.multiple_of((1 - c) * HCH + k * SUB, SUB), SUB)
            carried[:, cols] = c_in[k].astype(F32)

    def ssm_finish(n):
        cols = pl.ds(pl.multiple_of(n * WIDE, WIDE), WIDE)
        state = (carried[:, cols] * dexp[0:1, cols]).astype(BF)
        state = jnp.concatenate([jnp.zeros((STATE, WIDE), BF), state], axis=0)
        mixed = (
            jnp.dot(amat[...], xw[:, cols], preferred_element_type=F32)
            + jnp.dot(plo[0], state, preferred_element_type=F32)
            + jnp.dot(plo[1], state, preferred_element_type=F32)
        )
        ssm_ref[:, cols] = (
            gain[:, cols] * mixed + sexp[0:1, cols] * x_ref[:, cols].astype(F32)
        ).astype(BF)

    def assemble():
        blocks_all().wait_recv()
        context = jnp.dot(compact[...], arrived[...], preferred_element_type=F32).astype(BF)
        buf[where_rows(1, me, 0)] = context[0:HALF]
        buf[where_rows(1, me, 1)] = context[HALF:TOK]
        send_own(1)

    def stage(k):
        is_ctx = (k == 3) | (k >= 5)
        s = jnp.where(k < 3, k + 1, jnp.where(k == 3, 1, jnp.where(k == 4, 4, k - 3)))
        return jnp.where(is_ctx, 1, 0), s

    turn = 8 + (18 * z) // 7

    def step(fine, _):
        it = fine // 2
        kind = lax.rem(fine, 2)
        early = kind == 0
        k = it // 2
        j = lax.rem(it, 2)
        array, s = stage(k)
        turned = jnp.where(s == 4, 1 - j, j)
        last = 4 - turned

        @pl.when(fine == READY)
        def _():
            assemble()

        @pl.when((s <= last) & (k < 7))
        def _():
            half = jnp.where(early, turned, 1 - turned)
            origin = jnp.where(early, right_origin(s), left_origin(s)) + c
            kv_copy(array, kind, s, half, origin, sib).wait_recv()

            @pl.when(s < last)
            def _():
                kv_copy(array, kind, s + 1, half, origin, jnp.where(early, right, left)).start()

            kv_copy(array, 2 + kind, s, half, origin, sib).start()

        @pl.when(fine == 1)
        def _():
            hand_out()

        @pl.when((fine >= 1) & (fine <= 3))
        def _():
            lax.fori_loop(5 * fine - 4, 5 * fine + 1, give, 0)

        @pl.when((fine <= 6) & (fine != 1))
        def _():
            widen(jnp.where(fine == 0, 2, fine + 1), 0)

        @pl.when(fine == 6)
        def _():
            share_ends()

        @pl.when(fine == 7)
        def _():
            own_keys()

        @pl.when(fine == turn)
        def _():
            chain()

        @pl.when(fine == turn + 3)
        def _():
            ssm_ready()

        @pl.when((fine >= turn + 3) & (fine < turn + 3 + CH // WIDE))
        def _():
            ssm_finish(fine - turn - 3)

        parray, ps = stage(k - 1)
        own = (k - 1 == 4) & (j == 1)
        uarray = jnp.where(own, 1, parray)
        chip = jnp.where(
            own, z, lax.rem(jnp.where(j == 0, z + NZ - ps, z + ps), NZ)
        )

        @pl.when(it >= 2)
        def _():
            @pl.when(own & early)
            def _():
                for half in range(2):
                    kv_copy(1, 2, 0, half, sib, sib).wait_recv()

            @pl.when(jnp.logical_not(own) & (ps < 4) & early)
            def _():
                for half in range(2):
                    kv_copy(
                        parray, 2 + j, ps, half,
                        jnp.where(j == 0, right_origin(ps), left_origin(ps)) + 1 - c, sib,
                    ).wait_recv()

            @pl.when(jnp.logical_not(own) & (ps == 4) & early)
            def _():
                sib_wait(parray, 0, 4, 0)
                sib_wait(parray, 1, 4, 1)

            for part in range(2):

                @pl.when(((uarray == 1) | (chip < z)) & (kind == part))
                def _():
                    attend(
                        pl.multiple_of(uarray * 2048 + chip * UNIT, UNIT),
                        jnp.where(uarray == 1, length - chip * UNIT, UNIT),
                        None,
                        (2 * part, 2 * part + 1),
                    )

        return 0

    lax.fori_loop(0, 32, step, 0)

    for kind in range(2):
        origin = (right_origin(4) if kind == 0 else left_origin(4)) + c
        kv_copy(1, kind, 4, kind, origin, sib).wait_recv()
        kv_copy(1, 2 + kind, 4, kind, origin, sib).start()

    def rest(n, _):
        ssm_finish(n)
        return 0

    lax.fori_loop(jnp.minimum(CH // WIDE, 32 - turn - 3), CH // WIDE, rest, 0)
    ssm_store.start()
    sib_wait(1, 0, 4, 0)
    sib_wait(1, 1, 4, 1)
    final = lax.rem(z + 4, NZ)
    attend(pl.multiple_of(2048 + final * UNIT, UNIT), length - final * UNIT, None, range(KVH))
    for g in range(KVH):
        sums = acc[g]
        done = (sums[:, 0:DIM] / sums[:, DIM:2 * DIM]).astype(BF)
        for j in range(GRP):
            h = g * GRP + j
            att_ref[:, h * DIM:(h + 1) * DIM] = done[j * TOK:(j + 1) * TOK]

    att_store.start()

    sent = buf.at[pl.ds(0, 60 * HALF)]
    pltpu.make_async_remote_copy(
        src_ref=sent, dst_ref=sent, send_sem=ksend.at[0], recv_sem=krecv.at[0],
        device_id=(sib, ex), device_id_type=MESH,
    ).wait_send()
    ids_y().wait_send()
    ids_x().wait_send()
    blocks_all().wait_send()
    e_copy().wait_send()
    d_copy().wait_send()
    ssm_store.wait()
    att_store.wait()
    for k in range(NSUB):
        c_copy(k).wait_send()

        @pl.when(z < NZ - 1)
        def _():
            p_copy(k).wait_send()


def local(
    queries, new_kv, kv_pool, holders, slots, lengths,
    ssm_input, step_sizes, projections, decay_rates, skip_gain, init_state,
):
    kv = new_kv[0]
    pool = kv_pool.reshape(256, 2, 512)
    vmem = pl.BlockSpec(memory_space=pltpu.VMEM)
    far = pl.BlockSpec(memory_space=pl.ANY)
    smem = pl.BlockSpec(memory_space=pltpu.SMEM)
    dma = pltpu.SemaphoreType.DMA
    attended, ssm_out = pl.pallas_call(
        kernel,
        out_shape=(
            jax.ShapeDtypeStruct((TOK, 4096), BF),
            jax.ShapeDtypeStruct((TOK, CH), BF),
        ),
        in_specs=[far, vmem, far, vmem, vmem, smem, far] + [vmem] * 4 + [far],
        out_specs=(far, far),
        scratch_shapes=[
            pltpu.VMEM((TOK, 4096), BF),
            pltpu.VMEM((256, 2, 512), BF),
            pltpu.VMEM((TOK, 1024), BF),
            pltpu.VMEM((256, 1024), BF),
            pltpu.VMEM((TOK, CH), BF),
            pltpu.VMEM((128, 1024), F32),
            pltpu.VMEM((TOK, 4096), BF),
            pltpu.VMEM((TOK, CH), BF),
            pltpu.VMEM((32 * TOK, 1024), BF),
            pltpu.VMEM((KVH, GRP * TOK, DIM), BF),
            pltpu.VMEM((KVH, GRP * TOK, DIM), F32),
            pltpu.VMEM((KVH, GRP * TOK, 2 * DIM), F32),
            pltpu.VMEM((SIDE, 64, 128), I32),
            pltpu.VMEM((SIDE, 64, 128), I32),
            pltpu.VMEM((SIDE, 64, 128), I32),
            pltpu.VMEM((256, 1024), BF),
            pltpu.VMEM((256, 1024), BF),
            pltpu.VMEM((128, 256), BF),
            pltpu.VMEM((TOK, CH), BF),
            pltpu.VMEM((TOK, CH), F32),
            pltpu.VMEM((8, CH), F32),
            pltpu.VMEM((8, CH), F32),
            pltpu.VMEM((STATE, CH), F32),
            pltpu.VMEM((128, 128), BF),
            pltpu.VMEM((2, 128, 32), BF),
            pltpu.VMEM((STATE, HCH), BF),
            pltpu.VMEM((STATE, HCH), BF),
            pltpu.VMEM((8, HCH), F32),
            pltpu.VMEM((NSUB, STATE, SUB), BF),
            pltpu.VMEM((NSUB, STATE, SUB), BF),
            pltpu.VMEM((NSUB, STATE, SUB), BF),
            pltpu.VMEM((NSUB, STATE, SUB), BF),
            pltpu.VMEM((STATE, CH), F32),
            dma((1,)), dma((80,)),
            dma((2,)), dma((2,)),
            dma((1,)), dma((1,)),
            dma((2,)), dma((2,)),
            dma((NSUB,)), dma((NSUB,)),
            dma((NSUB,)), dma((NSUB,)),
            dma((6,)),
        ],
        compiler_params=pltpu.CompilerParams(
            vmem_limit_bytes=58 * 2 ** 20, collective_id=3, has_side_effects=True
        ),
        name="resume",
    )(
        queries[0], kv, pool, holders, slots, lengths,
        ssm_input[0], step_sizes[0], projections[0].T,
        decay_rates[None], skip_gain[None], init_state[0],
    )
    return attended[None], ssm_out[None]


def solution(mesh):
    placed = (
        P("expert", "seq", None),
        P("expert", "seq", None, None),
        P(("seq", "expert"), None, None, None),
        P("expert", "seq"),
        P("expert", "seq"),
        P(),
        P("expert", "seq", None),
        P("expert", "seq", None),
        P("expert", "seq", None),
        P(),
        P(),
        P("expert", None, None),
    )
    return jax.shard_map(
        local,
        mesh=mesh,
        in_specs=placed,
        out_specs=(P("expert", "seq", None), P("expert", "seq", None)),
        check_vma=False,
    )
```
